256 devices in a mesh: section: 16 (over x_hi, z), dp: 16 (over y, x_lo, core).
Axes of the slice: x: 4 (x_hi: 2, x_lo: 2; x = x_hi * 2 + x_lo), y: 4, z: 8, core: 2. Of those that a mesh axis runs over, the one named last changes fastest.
Arguments:
- weight: bfloat16 [16, 2048, 2048], P('section', 'dp'), may hold values from -0.125 to 0.125
- gain: float32 [16, 2048], P('section'), may hold values from 0.1 to 1.9
- acts_in: bfloat16 [16, 2048, 2048], P('section', 'dp'), may hold values from -6 to 6
- grads_in: bfloat16 [16, 2048, 2048], P('section', 'dp'), may hold values from -0.59765625 to 0.59765625
- parked: bfloat16 [16, 3, 2048, 2048], P('section', None, 'dp'), may hold values from -6 to 6
- fetch_slot: int32 [16], replicated, may hold values from 0 to 2
- park_slot: int32 [16], replicated, may hold values from 0 to 2
Outputs:
- next_acts: bfloat16 [16, 2048, 2048], P('section', 'dp')
- next_grads: bfloat16 [16, 2048, 2048], P('section', 'dp')
- parked_out: bfloat16 [16, 3, 2048, 2048], P('section', None, 'dp')
- weight_grad: float32 [16, 2048, 2048], P('section', 'dp')
- gain_grad: float32 [16, 2048], P('section', 'dp')
The draws below stay inside these ranges and needn't reach their ends.
All inputs are finite; a program needn't handle non-finite values.
Results may differ from the reference program's by a relative error of at most 0.02.
Values may be sent and summed in bfloat16 or wider, within the bound.
No kernel may reach another device: no remote copies, remote signals or barrier semaphores. Data moves between devices by JAX's collectives and lax.ppermute only.
A program may use at most 64 MiB of HBM per device.

```python
import jax
import jax.numpy as jnp
from jax import lax

D = 2048
TOK_DEV = 128
SLOTS = 3
TOKENS = 2048
SECTIONS = 16
N_DP = 16


def set_ends(entries, rng, smallest, top_value):
    spot = [jax.random.randint(jax.random.fold_in(rng, axis), (), 0, length) for axis, length in enumerate(entries.shape)]
    widest = entries.shape.index(max(entries.shape))
    next_to = spot[:widest] + [(spot[widest] + 1) % entries.shape[widest]] + spot[widest + 1:]
    return entries.at[tuple(spot)].set(smallest).at[tuple(next_to)].set(top_value)


def with_spikes(result, key, source, target, shards_of, factor):
    def block_of(dim):
        return (jnp.arange(result.shape[dim]) // (result.shape[dim] // shards_of)).reshape((-1,) + (1,) * (result.ndim - 1 - dim))

    first = jax.random.permutation(key, shards_of)[block_of(target)]
    other_side = (block_of(target) + shards_of // 2) % shards_of
    return jnp.where((block_of(source) == first) | (block_of(source) == other_side), factor * result, result)


def steps_of(stream_key, shape, split, least, largest):
    factor_of, own = 1.0, jax.random.fold_in(stream_key, 6)
    for axis_at, blocks in split:
        steps = jnp.exp(jax.random.uniform(jax.random.fold_in(own, axis_at), (blocks,), jnp.float32, least / len(split), largest / len(split)))
        factor_of = factor_of * jnp.repeat(steps, shape[axis_at] // blocks).reshape([-1 if axis == axis_at else 1 for axis in range(len(shape))])
    return factor_of


def centred(own_key, shape, scale, reach, split=(), dtype=jnp.bfloat16):
    loudness = steps_of(own_key, shape, split, -0.22, 0.18) if split else 1.0
    values = jax.random.normal(own_key, shape, jnp.float32) * scale * loudness
    return jnp.minimum(jnp.maximum(values, -reach), reach).astype(dtype)


def noise_with(stream_key, dims, deviation, limit, pieces, heavy, held_as=jnp.bfloat16):
    drawn = deviation * jax.random.normal(stream_key, dims, jnp.float32)
    if pieces:
        drawn = drawn * steps_of(stream_key, dims, pieces, -0.22, 0.18)
    return jnp.clip(with_spikes(drawn, jax.random.fold_in(stream_key, 3), *heavy), -limit, limit).astype(held_as)


def setup_inputs(seed: int = 0) -> dict:
    keys = jax.random.split(jax.random.key(seed), 8)
    return {
        "weight": centred(keys[0], (SECTIONS, D, D), D ** -0.5, 0.125, ((0, 16), (1, 16))),
        "gain": jnp.clip(1.0 + 0.18 * jax.random.normal(keys[1], (SECTIONS, D), jnp.float32), 0.1, 1.9),
        "acts_in": centred(keys[2], (SECTIONS, TOKENS, D), 1.0, 6.0, ((0, 16), (1, 16))),
        "grads_in": centred(keys[3], (SECTIONS, TOKENS, D), 0.1, 0.59765625, ((0, 16), (1, 16))),
        "parked": noise_with(keys[4], (SECTIONS, SLOTS, TOKENS, D), 1.0, 6.0, ((0, 16), (2, 16)), (2, 3, 16, 2.0)),
        "fetch_slot": set_ends(jax.random.randint(keys[5], (SECTIONS,), 0, SLOTS), jax.random.fold_in(keys[5], 1), 0, SLOTS - 1).astype(jnp.int32),
        "park_slot": set_ends(jax.random.randint(keys[6], (SECTIONS,), 0, SLOTS), jax.random.fold_in(keys[6], 1), 0, SLOTS - 1).astype(jnp.int32),
    }


EPSILON = 1e-05

def forward_rows(acts, gain_row, weight_mat):
    values = acts.astype(jnp.float32)
    inv_rms = lax.rsqrt(lax.optimization_barrier(jnp.mean(values * values, -1, keepdims=True)) + EPSILON)
    normed = (values * inv_rms * gain_row).astype(jnp.bfloat16)
    pre_act = jnp.dot(normed, weight_mat, preferred_element_type=jnp.float32)
    return (values + jax.nn.silu(pre_act)).astype(jnp.bfloat16)

def backward_rows(panel, grads, gain_row, weight_mat):
    values = panel.astype(jnp.float32)
    inv_rms = lax.rsqrt(lax.optimization_barrier(jnp.mean(values * values, -1, keepdims=True)) + EPSILON)
    unit_rows = values * inv_rms
    normed = (unit_rows * gain_row).astype(jnp.bfloat16)
    pre_act = jnp.dot(normed, weight_mat, preferred_element_type=jnp.float32)
    sigma = jax.nn.sigmoid(pre_act)
    grad_f = grads.astype(jnp.float32)
    delta = (grad_f * sigma * (1.0 + pre_act * (1.0 - sigma))).astype(jnp.bfloat16)
    back_rows = lax.dot_general(delta, weight_mat, (((1,), (1,)), ((), ())), preferred_element_type=jnp.float32)
    through = back_rows * gain_row
    grad_acts = (grad_f + inv_rms * (through - unit_rows * lax.optimization_barrier(jnp.mean(through * unit_rows, -1, keepdims=True)))).astype(jnp.bfloat16)
    return (grad_acts, normed, delta, back_rows * unit_rows)

def round_trip(value):
    return lax.optimization_barrier(value.astype(jnp.bfloat16)).astype(jnp.float32)

def section_terms(inputs):
    acts, grads, panel, gain_row, weight_mat = inputs
    out_rows = forward_rows(acts, gain_row, weight_mat)
    grad_acts, normed, delta, gain_rows = backward_rows(panel, grads, gain_row, weight_mat)
    width = weight_mat.shape[0]
    blocks = (normed.reshape(N_DP, TOK_DEV, width), delta.reshape(N_DP, TOK_DEV, width), gain_rows.reshape(N_DP, TOK_DEV, width))

    def add_block(carry, block):
        normed_blk, delta_blk, gain_blk = block
        part_w = lax.dot_general(normed_blk, delta_blk, (((0,), (0,)), ((), ())), preferred_element_type=jnp.float32)
        part_g = lax.optimization_barrier(jnp.sum(gain_blk, 0))
        return ((carry[0] + round_trip(part_w), carry[1] + round_trip(part_g)), None)
    init = (jnp.zeros((width, width), jnp.float32), jnp.zeros((width,), jnp.float32))
    sums, _ = lax.scan(add_block, init, blocks)
    return (out_rows, grad_acts, sums[0], sums[1])

def reference(weight, gain, acts_in, grads_in, parked, fetch_slot, park_slot):
    sections = weight.shape[0]
    mirrors = (sections - 1 - jnp.arange(sections)).astype(jnp.int32)
    panels = parked[mirrors, fetch_slot.astype(jnp.int32)]
    outs, grad_x, weight_grad, gain_grad = lax.map(section_terms, (acts_in, grads_in, panels, gain, weight))
    next_acts = jnp.roll(outs, 1, axis=0)
    next_grads = jnp.roll(grad_x, -1, axis=0)
    parked_out = parked.at[mirrors, park_slot.astype(jnp.int32)].set(acts_in)
    return (next_acts, next_grads, parked_out, weight_grad, gain_grad)
```

```python
import jax
import jax.numpy as jnp
from jax import lax
from jax.sharding import PartitionSpec as P

EPSILON = 1e-05


def mirrored(block, axis):
    count = lax.axis_size(axis)
    return lax.ppermute(block, axis, [(i, count - 1 - i) for i in range(count)])


def shifted(block, axis, distance):
    devices = range(lax.axis_size(axis))
    route = [((i - distance) % len(devices), i) for i in devices]
    return lax.ppermute(block, axis, route)


def forward_rows(acts, gain_row, weight_mat):
    values = acts.astype(jnp.float32)
    inv_rms = lax.rsqrt(jnp.mean(values * values, -1, keepdims=True) + EPSILON)
    normed = (values * inv_rms * gain_row).astype(jnp.bfloat16)
    pre_act = jnp.dot(normed, weight_mat, preferred_element_type=jnp.float32)
    return (values + jax.nn.silu(pre_act)).astype(jnp.bfloat16)


def shards(weight, gain, acts_in, grads_in, parked, fetch_slot, park_slot):
    sections = lax.axis_size("section")
    position = lax.axis_index("section")
    member = lax.axis_index("dp")
    partner = sections - 1 - position
    held = parked[0]
    tokens, width = acts_in.shape[1:]
    own_width = weight.shape[1]
    send_slot = lax.dynamic_index_in_dim(fetch_slot, partner, 0, keepdims=False)
    write_slot = lax.dynamic_index_in_dim(park_slot, partner, 0, keepdims=False)
    gain_row = gain[0]

    panel = mirrored(lax.dynamic_index_in_dim(held, send_slot, 0, keepdims=False), "section")
    full_weight = lax.all_gather(weight[0], "dp", axis=0, tiled=True)
    stashed = mirrored(acts_in[0], "section")

    values = panel.astype(jnp.float32)
    inv_rms = lax.rsqrt(jnp.mean(values * values, -1, keepdims=True) + EPSILON)
    unit_rows = values * inv_rms
    normed = (unit_rows * gain_row).astype(jnp.bfloat16)
    own_units = lax.all_to_all(
        unit_rows.astype(jnp.bfloat16), "dp", split_axis=1, concat_axis=0, tiled=True
    )
    pre_act = jnp.dot(normed, full_weight, preferred_element_type=jnp.float32)
    sigma = jax.nn.sigmoid(pre_act)
    grad_f = grads_in[0].astype(jnp.float32)
    delta = (grad_f * sigma * (1.0 + pre_act * (1.0 - sigma))).astype(jnp.bfloat16)
    all_delta = lax.all_gather(delta, "dp", axis=0, tiled=True)

    out_rows = forward_rows(acts_in[0], gain_row, full_weight)
    next_acts = shifted(out_rows, "section", 1)

    back_rows = lax.dot_general(
        delta, full_weight, (((1,), (1,)), ((), ())), preferred_element_type=jnp.float32
    )
    through = back_rows * gain_row
    grad_acts = (
        grad_f + inv_rms * (through - unit_rows * jnp.mean(through * unit_rows, -1, keepdims=True))
    ).astype(jnp.bfloat16)
    next_grads = shifted(grad_acts, "section", -1)
    parked_out = lax.dynamic_update_index_in_dim(held, stashed, write_slot, 0)

    outer = lax.dot_general(
        own_units, all_delta, (((0,), (0,)), ((), ())), preferred_element_type=jnp.float32
    )
    own_gain = lax.dynamic_slice_in_dim(gain_row, member * own_width, own_width)
    weight_grad = outer * own_gain[:, None]
    gain_grad = jnp.sum(outer * weight[0].astype(jnp.float32), -1)
    return (next_acts[None], next_grads[None], parked_out[None], weight_grad[None], gain_grad[None])


def solution(mesh):
    return jax.shard_map(
        shards,
        mesh=mesh,
        in_specs=(
            P("section", "dp", None),
            P("section", None),
            P("section", "dp", None),
            P("section", "dp", None),
            P("section", None, "dp", None),
            P(),
            P(),
        ),
        out_specs=(
            P("section", "dp", None),
            P("section", "dp", None),
            P("section", None, "dp", None),
            P("section", "dp", None),
            P("section", "dp"),
        ),
        check_vma=False,
    )
```

```python
import functools

import jax
import jax.numpy as jnp
from jax import lax
from jax.experimental import pallas as pl
from jax.experimental.pallas import tpu as pltpu
from jax.sharding import PartitionSpec as P

EPSILON = 1e-05
RING, PAIR, CORES = 4, 2, 2
CHIPS = RING * PAIR
MEMBERS = CHIPS * CORES
BLOCK = 128
TILE = 256

VMEM = pl.BlockSpec(memory_space=pltpu.VMEM)
SMEM = pl.BlockSpec(memory_space=pltpu.SMEM)
ANY = pl.BlockSpec(memory_space=pl.ANY)
F32, BF16 = jnp.float32, jnp.bfloat16


def struct(shape, dtype):
    return jax.ShapeDtypeStruct(shape, dtype)


def call(kernel, outs, args, specs, out_specs=None, scratch=(), flops=0, megabytes=32):
    nbytes = sum(a.size * a.dtype.itemsize for a in list(args) + list(outs))
    return pl.pallas_call(
        kernel,
        out_shape=list(outs),
        in_specs=list(specs),
        out_specs=list(out_specs) if out_specs else [VMEM] * len(outs),
        scratch_shapes=list(scratch),
        cost_estimate=pl.CostEstimate(flops=flops, bytes_accessed=nbytes, transcendentals=0),
        compiler_params=pltpu.CompilerParams(vmem_limit_bytes=megabytes * 1024 * 1024),
    )(*args)


def mirrored(block):
    count = lax.axis_size("section")
    return lax.ppermute(block, "section", [(i, count - 1 - i) for i in range(count)])


def shifted(block, distance):
    count = lax.axis_size("section")
    return lax.ppermute(block, "section", [((i - distance) % count, i) for i in range(count)])


def hop(block, ring=0, pair=0, core=0):
    route = []
    for i in range(MEMBERS):
        y, x, c = i // (PAIR * CORES), i // CORES % PAIR, i % CORES
        route.append((i, (((y + ring) % RING) * PAIR + (x ^ pair)) * CORES + (c ^ core)))
    return lax.ppermute(block, "dp", route)


def gathered(own):
    rows = own.shape[0] // 2
    pair = hop(own, pair=1)
    below = hop(own, ring=1)
    above = hop(own, ring=-1)
    far_low = hop(below[:rows], ring=1)
    far_high = hop(above[rows:], ring=-1)
    pair_below = hop(pair, ring=1)
    pair_above = hop(pair, ring=-1)
    pair_far_low = hop(far_low, pair=1)
    pair_far_high = hop(far_high, pair=1)
    early = [(0, 0, [own]), (0, 1, [pair]), (-1, 0, [below]), (1, 0, [above])]
    late = [
        (2, 0, [far_low, far_high]),
        (-1, 1, [pair_below]),
        (1, 1, [pair_above]),
        (2, 1, [pair_far_low, pair_far_high]),
    ]
    return early, late


def place():
    member = lax.axis_index("dp")
    core = lax.rem(member, CORES)
    return member, core


def chip_of(up, other):
    member = lax.axis_index("dp")
    ring_at = lax.div(member, PAIR * CORES)
    pair_at = lax.rem(lax.div(member, CORES), PAIR)
    pair_to = 1 - pair_at if other else pair_at
    return lax.rem(ring_at + up + RING, RING) * PAIR + pair_to


def columns_of(step):
    return pl.ds(pl.multiple_of(step * TILE, TILE), TILE)


def inverse_rms(values):
    return lax.rsqrt(jnp.mean(values * values, -1, keepdims=True) + EPSILON)


def fetch_kernel(slots, held, out, sem):
    partner = lax.axis_size("section") - 1 - lax.axis_index("section")
    copy = pltpu.make_async_copy(held.at[0, slots[partner]], out, sem)
    copy.start()
    copy.wait()


def normed_kernel(rows, gain, mine, send, *units):
    _, core = place()
    values = rows[...].astype(F32)
    unit = values * inverse_rms(values)
    normed = (unit * gain[...]).astype(BF16)
    for chip in range(CHIPS):
        at = chip * CORES * BLOCK
        first, second = normed[:, at : at + BLOCK], normed[:, at + BLOCK : at + 2 * BLOCK]
        mine[chip] = jnp.where(core == 0, first, second)
        send[chip] = jnp.where(core == 0, second, first)
        if units:
            first = jnp.transpose(unit[:, at : at + BLOCK]).astype(BF16)
            second = jnp.transpose(unit[:, at + BLOCK : at + 2 * BLOCK]).astype(BF16)
            units[0][chip, 0] = jnp.where(core == 0, first, second)
            units[0][chip, 1] = jnp.where(core == 0, second, first)


def product_kernel(layout, stacked, added, *refs):
    refs = list(refs)
    left = refs.pop()
    out_own, out_other = refs[-2:]
    del refs[-2:]
    if stacked:
        both = refs.pop(0)
        own, other = (lambda chip: both[chip, 0]), (lambda chip: both[chip, 1])
    else:
        own_ref, other_ref = refs.pop(0), refs.pop(0)
        own, other = (lambda chip: own_ref[chip]), (lambda chip: other_ref[chip])
    totals = [refs.pop(), refs.pop()][::-1] if added else None
    for k, (up, to_other, _) in enumerate(layout):
        chip = chip_of(up, to_other)
        left[:BLOCK, k * BLOCK : (k + 1) * BLOCK] = own(chip)
        left[BLOCK:, k * BLOCK : (k + 1) * BLOCK] = other(chip)

    @pl.loop(0, out_own.shape[1] // TILE)
    def _(step):
        columns = columns_of(step)
        right = jnp.concatenate([part[:, columns] for part in refs], 0)
        result = jnp.dot(left[...], right, preferred_element_type=F32)
        low, high = result[:BLOCK], result[BLOCK:]
        if added:
            low, high = low + totals[0][:, columns], high + totals[1][:, columns]
        out_own[:, columns] = low
        out_other[:, columns] = high


def product(blocks, chunks, totals=()):
    parts = [part for chunk in chunks for part in chunk[2]]
    layout = [(up, other, len(p)) for up, other, p in chunks]
    depth, width = len(chunks) * BLOCK, parts[0].shape[1]
    args = [*blocks, *parts, *totals]
    out = struct((BLOCK, width), F32)
    return call(
        functools.partial(product_kernel, layout, len(blocks) == 1, bool(totals)),
        [out, out],
        args,
        [VMEM] * len(args),
        scratch=[pltpu.VMEM((2 * BLOCK, depth), BF16)],
        flops=2 * 2 * BLOCK * depth * width,
    )


def delta_kernel(own, received, grads, delta):
    @pl.loop(0, delta.shape[1] // TILE)
    def _(step):
        columns = columns_of(step)
        pre_act = own[:, columns] + received[:, columns]
        sigma = jax.nn.sigmoid(pre_act)
        grad_f = grads[:, columns].astype(F32)
        delta[:, columns] = (grad_f * sigma * (1.0 + pre_act * (1.0 - sigma))).astype(BF16)


def out_kernel(own, received, acts, out):
    @pl.loop(0, out.shape[1] // TILE)
    def _(step):
        columns = columns_of(step)
        pre_act = own[:, columns] + received[:, columns]
        values = acts[:, columns].astype(F32)
        out[:, columns] = (values + pre_act * jax.nn.sigmoid(pre_act)).astype(BF16)


def back_kernel(layout, delta_own, delta_other, *refs):
    refs = list(refs)
    left = refs.pop()
    back_own, back_other = refs[-2:]
    left[:BLOCK] = delta_own[...]
    left[BLOCK:] = delta_other[...]
    at = 0
    for k in range(0, len(layout), 2):
        parts = []
        for _, _, count in layout[k : k + 2]:
            parts += [refs[at + i][...] for i in range(count)]
            at += count
        right = jnp.concatenate(parts, 0)
        result = lax.dot_general(
            left[...], right, (((1,), (1,)), ((), ())), preferred_element_type=F32
        )
        for i, (up, other, _) in enumerate(layout[k : k + 2]):
            chip = chip_of(up, other)
            back_own[chip] = result[:BLOCK, i * BLOCK : (i + 1) * BLOCK]
            back_other[chip] = result[BLOCK:, i * BLOCK : (i + 1) * BLOCK]


def grad_kernel(panel, gain, grads, back_own, back_received, grad_acts, through):
    _, core = place()
    values = panel[...].astype(F32)
    inverse = inverse_rms(values)
    for chip in range(CHIPS):
        at = chip * CORES * BLOCK
        own, received = back_own[chip], back_received[chip]
        through[:, at : at + BLOCK] = jnp.where(core == 0, own, received)
        through[:, at + BLOCK : at + 2 * BLOCK] = jnp.where(core == 0, received, own)
    unit = values * inverse
    scaled = through[...] * gain[...]
    mean = jnp.mean(scaled * unit, -1, keepdims=True)
    grad_acts[...] = (grads[...].astype(F32) + inverse * (scaled - unit * mean)).astype(BF16)


def park_kernel(slots, held, stashed, out, sems):
    partner = lax.axis_size("section") - 1 - lax.axis_index("section")
    slot = slots[partner]
    for k in range(held.shape[1]):

        @pl.when(slot == k)
        def _(k=k):
            pltpu.make_async_copy(stashed, out.at[0, k], sems.at[k]).start()

        @pl.when(slot != k)
        def _(k=k):
            pltpu.make_async_copy(held.at[0, k], out.at[0, k], sems.at[k]).start()

    for k in range(held.shape[1]):
        pltpu.make_async_copy(stashed, out.at[0, k], sems.at[k]).wait()


def finish_kernel(
    own, received, weight, gain, acts, grads, weight_grad, gain_grad, next_acts, next_grads, sems
):
    member, _ = place()
    copies = [
        pltpu.make_async_copy(acts, next_acts.at[0], sems.at[0]),
        pltpu.make_async_copy(grads, next_grads.at[0], sems.at[1]),
    ]
    for copy in copies:
        copy.start()
    own_gain = gain[:, pl.ds(pl.multiple_of(member * BLOCK, BLOCK), BLOCK)]
    scale = jnp.transpose(jnp.broadcast_to(own_gain, (BLOCK, BLOCK)))[:, :1]
    total = jnp.zeros((BLOCK, 1), F32)
    for at in range(0, own.shape[1], TILE):
        outer = own[:, at : at + TILE] + received[:, at : at + TILE]
        weight_grad[0, :, at : at + TILE] = outer * scale
        total += jnp.sum(outer * weight[0, :, at : at + TILE].astype(F32), -1, keepdims=True)
    gain_grad[...] = jnp.transpose(jnp.broadcast_to(total, (BLOCK, BLOCK)))[:1]
    for copy in copies:
        copy.wait()


def shards(weight, gain, acts_in, grads_in, parked, fetch_slot, park_slot):
    tokens, width = acts_in.shape[1:]
    acts, grads = acts_in[0], grads_in[0]
    rows, blocks = struct((tokens, width), BF16), struct((CHIPS, BLOCK, BLOCK), BF16)
    sent_rows = struct((tokens, width), BF16)
    back = struct((CHIPS, BLOCK, BLOCK), F32)

    (fetched,) = call(
        fetch_kernel, [sent_rows], [fetch_slot, parked], [SMEM, ANY], [ANY], [pltpu.SemaphoreType.DMA]
    )
    panel = mirrored(fetched)
    early, late = gathered(weight[0])
    stashed = mirrored(acts)

    mine, send = call(normed_kernel, [blocks, blocks], [acts, gain], [VMEM] * 2)
    forward = [mine, hop(send, core=1)]
    pre = product(forward, early)
    pre_own, pre_other = product(forward, late, pre)

    mine, send, units = call(
        normed_kernel,
        [blocks, blocks, struct((CHIPS, CORES, BLOCK, BLOCK), BF16)],
        [panel, gain],
        [VMEM] * 2,
    )
    backward = [mine, hop(send, core=1)]
    panel_pre = product(backward, early)
    panel_own, panel_other = product(backward, late, panel_pre)
    units = lax.all_to_all(
        units,
        "dp",
        split_axis=0,
        concat_axis=0,
        tiled=True,
        axis_index_groups=[[chip * CORES + c for chip in range(CHIPS)] for c in range(CORES)],
    )

    (delta,) = call(
        delta_kernel, [rows], [panel_own, hop(panel_other, core=1), grads], [VMEM] * 3
    )
    delta_early, delta_late = gathered(delta)

    (out_rows,) = call(
        out_kernel, [rows], [pre_own, hop(pre_other, core=1), acts], [VMEM] * 3
    )
    next_acts = shifted(out_rows, 1)

    chunks = early + late
    parts = [part for chunk in chunks for part in chunk[2]]
    back_own, back_other = call(
        functools.partial(back_kernel, [(up, other, len(p)) for up, other, p in chunks]),
        [back, back],
        [delta, hop(delta, core=1), *parts],
        [VMEM] * (2 + len(parts)),
        scratch=[pltpu.VMEM((2 * BLOCK, width), BF16)],
        flops=2 * 2 * BLOCK * CHIPS * BLOCK * width,
    )
    (grad_acts,) = call(
        grad_kernel,
        [rows],
        [panel, gain, grads, back_own, hop(back_other, core=1)],
        [VMEM] * 5,
        scratch=[pltpu.VMEM((tokens, width), F32)],
    )
    next_grads = shifted(grad_acts, -1)
    (parked_out,) = call(
        park_kernel,
        [struct(parked.shape, BF16)],
        [park_slot, parked, stashed],
        [SMEM, ANY, ANY],
        [ANY],
        [pltpu.SemaphoreType.DMA((parked.shape[1],))],
    )

    outer = product([units], delta_early)
    outer_own, outer_other = product([units], delta_late, outer)
    weight_grad, gain_grad, next_acts, next_grads = call(
        finish_kernel,
        [
            struct((1, BLOCK, width), F32),
            struct((1, BLOCK), F32),
            struct((1, tokens, width), BF16),
            struct((1, tokens, width), BF16),
        ],
        [outer_own, hop(outer_other, core=1), weight, gain, next_acts, next_grads],
        [VMEM] * 4 + [ANY] * 2,
        [VMEM, VMEM, ANY, ANY],
        [pltpu.SemaphoreType.DMA((2,))],
    )
    return next_acts, next_grads, parked_out, weight_grad, gain_grad


def solution(mesh):
    return jax.shard_map(
        shards,
        mesh=mesh,
        in_specs=(
            P("section", "dp", None),
            P("section", None),
            P("section", "dp", None),
            P("section", "dp", None),
            P("section", None, "dp", None),
            P(),
            P(),
        ),
        out_specs=(
            P("section", "dp", None),
            P("section", "dp", None),
            P("section", None, "dp", None),
            P("section", "dp", None),
            P("section", "dp"),
        ),
        check_vma=False,
    )
```

```python
import functools

import jax
import jax.numpy as jnp
from jax import lax
from jax.experimental import pallas as pl
from jax.experimental.pallas import tpu as pltpu
from jax.sharding import PartitionSpec as P

EPSILON = 1e-05
RING, PAIR, CORES = 4, 2, 2
CHIPS = RING * PAIR
MEMBERS = CHIPS * CORES
BLOCK = 128
TILE = 256
MEGABYTES = 12
WIDTH = 2048

VMEM = pl.BlockSpec(memory_space=pltpu.VMEM)
SMEM = pl.BlockSpec(memory_space=pltpu.SMEM)
ANY = pl.BlockSpec(memory_space=pl.ANY)
F32, BF16 = jnp.float32, jnp.bfloat16


def struct(shape, dtype):
    return jax.ShapeDtypeStruct(shape, dtype)


def call(
    name, kernel, outs, args, specs, out_specs=None, scratch=(), flops=0, after=(), aliases=None
):
    nbytes = sum(a.size * a.dtype.itemsize for a in list(args) + list(outs))
    given = len(args)

    def body(*refs):
        kernel(*refs[:given], *refs[given + len(after) :])

    return pl.pallas_call(
        body,
        out_shape=list(outs),
        in_specs=list(specs) + [ANY] * len(after),
        out_specs=list(out_specs) if out_specs else [VMEM] * len(outs),
        scratch_shapes=list(scratch),
        input_output_aliases=aliases or {},
        name=name,
        cost_estimate=pl.CostEstimate(flops=flops, bytes_accessed=nbytes, transcendentals=0),
        compiler_params=pltpu.CompilerParams(vmem_limit_bytes=MEGABYTES * 1024 * 1024),
    )(*args, *after)


def mirrored(block):
    count = lax.axis_size("section")
    return lax.ppermute(block, "section", [(i, count - 1 - i) for i in range(count)])


def shifted(block, distance):
    count = lax.axis_size("section")
    return lax.ppermute(block, "section", [((i - distance) % count, i) for i in range(count)])


def hop(block, ring=0, pair=0, core=0):
    route = []
    for i in range(MEMBERS):
        y, x, c = i // (PAIR * CORES), i // CORES % PAIR, i % CORES
        route.append((i, (((y + ring) % RING) * PAIR + (x ^ pair)) * CORES + (c ^ core)))
    return lax.ppermute(block, "dp", route)


def gathered(own, after=(), take_after=()):
    rows, width = own.shape
    half = rows // 2
    with jax.named_scope("below"):
        below = hop(own, ring=1)
    with jax.named_scope("above"):
        above = hop(own, ring=-1)
    with jax.named_scope("pair"):
        pair = hop(own, pair=1)
    packed = struct((half + rows, width), own.dtype)
    up, down = call(
        "pack",
        pack_kernel,
        [packed, packed],
        [below, above, pair],
        [VMEM] * 3,
        scratch=[pltpu.SemaphoreType.DMA((4,))],
        after=after,
    )
    with jax.named_scope("up"):
        up = hop(up, ring=1)
    with jax.named_scope("down"):
        down = hop(down, ring=-1)
    halves = struct((half, width), own.dtype)
    low, high, token = call(
        "take",
        take_kernel,
        [halves, halves, struct((8, BLOCK), F32)],
        [up, down],
        [VMEM] * 2,
        scratch=[pltpu.SemaphoreType.DMA((2,))],
        after=take_after,
    )
    with jax.named_scope("far_up"):
        far_up = hop(low, ring=1)
    with jax.named_scope("far_down"):
        far_down = hop(high, ring=-1)
    near = [
        (0, 0, [(own, 0, rows)]),
        (-1, 0, [(below, 0, rows)]),
        (1, 0, [(above, 0, rows)]),
        (0, 1, [(pair, 0, rows)]),
    ]
    middle = [
        (2, 0, [(up, 0, half), (down, rows, rows + half)]),
        (-1, 1, [(up, half, half + rows)]),
        (1, 1, [(down, 0, rows)]),
    ]
    far = [(2, 1, [(far_up, 0, half), (far_down, 0, half)])]
    return near, middle, far, token


def arrays_of(chunks):
    arrays, layout = [], []
    for up, other, pieces in chunks:
        placed = []
        for array, first, last in pieces:
            at = next((i for i, a in enumerate(arrays) if a is array), len(arrays))
            if at == len(arrays):
                arrays.append(array)
            placed.append((at, first, last))
        layout.append((up, other, placed))
    return arrays, layout


def place():
    member = lax.axis_index("dp")
    core = lax.rem(member, CORES)
    return member, core


def chip_of(up, other):
    member = lax.axis_index("dp")
    ring_at = lax.div(member, PAIR * CORES)
    pair_at = lax.rem(lax.div(member, CORES), PAIR)
    pair_to = 1 - pair_at if other else pair_at
    return lax.rem(ring_at + up + RING, RING) * PAIR + pair_to


def columns_of(step):
    return pl.ds(pl.multiple_of(step * TILE, TILE), TILE)


def inverse_rms(values):
    return lax.rsqrt(jnp.mean(values * values, -1, keepdims=True) + EPSILON)


def split_kernel(slots, held, mine, send, panel, sem):
    _, core = place()
    partner = lax.axis_size("section") - 1 - lax.axis_index("section")
    copy = pltpu.make_async_copy(held.at[0, slots[partner]], panel, sem)
    copy.start()
    copy.wait()
    for chip in range(CHIPS):
        at, to = chip * CORES * BLOCK, chip * BLOCK
        first, second = panel[:, at : at + BLOCK], panel[:, at + BLOCK : at + 2 * BLOCK]
        mine[:, to : to + BLOCK] = jnp.where(core == 0, first, second)
        send[:, to : to + BLOCK] = jnp.where(core == 0, second, first)


def join_kernel(mine, received, joined):
    rows = mine.shape[0]
    joined[:rows] = mine[...]
    joined[rows:] = received[...]


def copy_all(pairs, sems):
    copies = [pltpu.make_async_copy(a, b, sems.at[i]) for i, (a, b) in enumerate(pairs)]
    for copy in copies:
        copy.start()
    return copies


def pack_kernel(below, above, pair, up, down, sems):
    rows = pair.shape[0]
    half = rows // 2
    copies = copy_all(
        [
            (pair, up.at[pl.ds(half, rows)]),
            (pair, down.at[pl.ds(0, rows)]),
            (below.at[pl.ds(0, half)], up.at[pl.ds(0, half)]),
            (above.at[pl.ds(half, half)], down.at[pl.ds(rows, half)]),
        ],
        sems,
    )
    for copy in copies:
        copy.wait()


def take_kernel(up, down, low, high, token, sems):
    token[...] = jnp.zeros_like(token)
    rows = low.shape[0]
    copies = copy_all([(up.at[pl.ds(rows, rows)], low), (down.at[pl.ds(rows, rows)], high)], sems)
    for copy in copies:
        copy.wait()


def units_kernel(half, received, keep, send, panel):
    member, core = place()
    pair_at = lax.rem(lax.div(member, CORES), PAIR)
    rows = received.shape[0]
    for chip in range(CHIPS):
        at, of = chip * CORES * BLOCK, chip * BLOCK
        own, other = half[:rows, of : of + BLOCK], received[:, of : of + BLOCK]
        panel[:, at : at + BLOCK] = jnp.where(core == 0, own, other)
        panel[:, at + BLOCK : at + 2 * BLOCK] = jnp.where(core == 0, other, own)
    values = panel[...].astype(F32)
    unit = values * inverse_rms(values)
    for y in range(RING):
        blocks = []
        for block in range(PAIR * CORES):
            at = (y * PAIR * CORES + block) * BLOCK
            blocks.append(jnp.transpose(unit[:, at : at + BLOCK]).astype(BF16))
        for c in range(CORES):
            mine = [jnp.where(core == 0, blocks[x + c], blocks[x + 1 - c]) for x in (0, CORES)]
            keep[y, c] = jnp.where(pair_at == 0, mine[0], mine[1])
            send[y, c] = jnp.where(pair_at == 0, mine[1], mine[0])


def mix_kernel(keep, received, mixed, token):
    token[...] = jnp.zeros_like(token)
    for y in range(RING):
        mixed[y, 0] = keep[y]
        mixed[y, 1] = received[y]


def normed_kernel(rows, gain, mine, send):
    _, core = place()
    values = rows[...].astype(F32)
    unit = values * inverse_rms(values)
    normed = (unit * gain[...]).astype(BF16)
    for chip in range(CHIPS):
        at = chip * CORES * BLOCK
        first, second = normed[:, at : at + BLOCK], normed[:, at + BLOCK : at + 2 * BLOCK]
        mine[chip] = jnp.where(core == 0, first, second)
        send[chip] = jnp.where(core == 0, second, first)


def product_kernel(layout, kind, added, *refs):
    refs = list(refs)
    left, token = refs.pop(), refs.pop(-1)
    token[...] = jnp.zeros_like(token)
    out_own, out_other = refs[-2:]
    del refs[-2:]
    _, core = place()
    first_ref, second_ref = refs.pop(0), None if kind == "stacked" else refs.pop(0)
    totals = [refs.pop(), refs.pop()][::-1] if added else None
    for k, (up, to_other, _) in enumerate(layout):
        chip = chip_of(up, to_other)
        columns = slice(k * BLOCK, (k + 1) * BLOCK)
        if kind == "stacked":
            left[:BLOCK, columns] = first_ref[lax.div(chip, PAIR), to_other, 0]
            left[BLOCK:, columns] = first_ref[lax.div(chip, PAIR), to_other, 1]
        elif kind == "pair":
            left[:BLOCK, columns] = first_ref[chip]
            left[BLOCK:, columns] = second_ref[chip]
        else:
            at = pl.ds(pl.multiple_of(chip * BLOCK, BLOCK), BLOCK)
            of = pl.ds(pl.multiple_of((chip * CORES + core) * BLOCK, BLOCK), BLOCK)
            left[:, columns] = (first_ref[:, at].astype(F32) * second_ref[:, of]).astype(BF16)

    @pl.loop(0, WIDTH // TILE)
    def _(step):
        columns = columns_of(step)
        right = jnp.concatenate(
            [refs[i][first:last, columns] for _, _, placed in layout for i, first, last in placed], 0
        )
        result = jnp.dot(left[...], right, preferred_element_type=F32)
        low, high = result[:BLOCK], result[BLOCK:]
        if added:
            low, high = low + totals[0][:, columns], high + totals[1][:, columns]
        out_own[:, columns] = low
        out_other[:, columns] = high.astype(out_other.dtype)

    if kind == "panel":
        if added:
            squares = totals[1][:, WIDTH:]
            rounded = squares.astype(BF16)
            out_own[:, WIDTH:] = totals[0][:, WIDTH:]
            out_other[:, WIDTH : WIDTH + BLOCK] = rounded
            out_other[:, WIDTH + BLOCK :] = (squares - rounded.astype(F32)).astype(BF16)
        else:
            values = first_ref[...].astype(F32)
            squares = jnp.broadcast_to(
                jnp.sum(values * values, -1, keepdims=True), (2 * BLOCK, BLOCK)
            )
            out_own[:, WIDTH:] = squares[:BLOCK]
            out_other[:, WIDTH:] = squares[BLOCK:]


def product(name, kind, blocks, chunks, totals=(), after=()):
    parts, layout = arrays_of(chunks)
    depth, width = len(chunks) * BLOCK, WIDTH + (BLOCK if kind == "panel" else 0)
    last = struct((BLOCK, width + (BLOCK if kind == "panel" else 0)), BF16)
    args = [*blocks, *parts, *totals]
    out = struct((BLOCK, width), F32)
    return call(
        name,
        functools.partial(product_kernel, layout, kind, bool(totals)),
        [out, last if totals else out, struct((8, BLOCK), F32)],
        args,
        [VMEM] * len(args),
        scratch=[pltpu.VMEM((2 * BLOCK, depth), BF16)],
        flops=2 * 2 * BLOCK * depth * width,
        after=after,
    )


def delta_kernel(own, received, grads, delta):
    squares = own[:, WIDTH : WIDTH + 1] + (
        received[:, WIDTH : WIDTH + 1].astype(F32)
        + received[:, WIDTH + BLOCK : WIDTH + BLOCK + 1].astype(F32)
    )
    inverse = lax.rsqrt(squares * (1.0 / WIDTH) + EPSILON)

    @pl.loop(0, WIDTH // TILE)
    def _(step):
        columns = columns_of(step)
        pre_act = (own[:, columns] + received[:, columns].astype(F32)) * inverse
        sigma = jax.nn.sigmoid(pre_act)
        grad_f = grads[:, columns].astype(F32)
        delta[:, columns] = (grad_f * sigma * (1.0 + pre_act * (1.0 - sigma))).astype(BF16)


def out_kernel(own, received, acts, out, token):
    token[...] = jnp.zeros_like(token)

    @pl.loop(0, out.shape[1] // TILE)
    def _(step):
        columns = columns_of(step)
        pre_act = own[:, columns] + received[:, columns].astype(F32)
        values = acts[:, columns].astype(F32)
        out[:, columns] = (values + pre_act * jax.nn.sigmoid(pre_act)).astype(BF16)


def back_kernel(layout, delta_own, delta_other, *refs):
    refs = list(refs)
    left = refs.pop()
    back_own, back_other = refs[-2:]
    left[:BLOCK] = delta_own[...]
    left[BLOCK:] = delta_other[...]
    for k in range(0, len(layout), 2):
        right = jnp.concatenate(
            [refs[i][first:last] for _, _, placed in layout[k : k + 2] for i, first, last in placed], 0
        )
        result = lax.dot_general(
            left[...], right, (((1,), (1,)), ((), ())), preferred_element_type=F32
        )
        for i, (up, other, _) in enumerate(layout[k : k + 2]):
            chip = chip_of(up, other)
            back_own[chip] = result[:BLOCK, i * BLOCK : (i + 1) * BLOCK]
            back_other[chip] = result[BLOCK:, i * BLOCK : (i + 1) * BLOCK]


def grad_kernel(panel, gain, grads, back_own, back_received, grad_acts, token, through):
    token[...] = jnp.zeros_like(token)
    _, core = place()
    values = panel[...].astype(F32)
    inverse = inverse_rms(values)
    for chip in range(CHIPS):
        at = chip * CORES * BLOCK
        own, received = back_own[chip], back_received[chip]
        through[:, at : at + BLOCK] = jnp.where(core == 0, own, received)
        through[:, at + BLOCK : at + 2 * BLOCK] = jnp.where(core == 0, received, own)
    unit = values * inverse
    scaled = through[...] * gain[...]
    mean = jnp.mean(scaled * unit, -1, keepdims=True)
    grad_acts[...] = (grads[...].astype(F32) + inverse * (scaled - unit * mean)).astype(BF16)


def keep_kernel(held, out, token, sem):
    copy = pltpu.make_async_copy(held, out, sem)
    copy.start()
    token[...] = jnp.zeros_like(token)
    copy.wait()


def park_kernel(slots, kept, stashed, out, token, sem):
    del kept
    partner = lax.axis_size("section") - 1 - lax.axis_index("section")
    copy = pltpu.make_async_copy(stashed, out.at[0, slots[partner]], sem)
    copy.start()
    token[...] = jnp.zeros_like(token)
    copy.wait()


def emit_kernel(acts, grads, next_acts, next_grads, token):
    next_acts[0] = acts[...]
    next_grads[0] = grads[...]
    token[...] = jnp.zeros_like(token)


def finish_kernel(own, received, weight, gain, weight_grad, gain_grad):
    member, _ = place()
    own_gain = gain[:, pl.ds(pl.multiple_of(member * BLOCK, BLOCK), BLOCK)]
    scale = jnp.transpose(jnp.broadcast_to(own_gain, (BLOCK, BLOCK)))[:, :1]
    total = jnp.zeros((BLOCK, 1), F32)
    for at in range(0, own.shape[1], TILE):
        outer = own[:, at : at + TILE] + received[:, at : at + TILE].astype(F32)
        weight_grad[0, :, at : at + TILE] = outer * scale
        total += jnp.sum(outer * weight[0, :, at : at + TILE].astype(F32), -1, keepdims=True)
    gain_grad[...] = jnp.transpose(jnp.broadcast_to(total, (BLOCK, BLOCK)))[:1]


def shards(weight, gain, acts_in, grads_in, parked, fetch_slot, park_slot):
    tokens, width = acts_in.shape[1:]
    acts, grads = acts_in[0], grads_in[0]
    rows, blocks = struct((tokens, width), BF16), struct((CHIPS, BLOCK, BLOCK), BF16)
    token = struct((8, BLOCK), F32)
    back = struct((CHIPS, BLOCK, BLOCK), F32)

    half = struct((tokens, width // CORES), BF16)
    mine, send = call(
        "split",
        split_kernel,
        [half, half],
        [fetch_slot, parked],
        [SMEM, ANY],
        scratch=[pltpu.VMEM((tokens, width), BF16), pltpu.SemaphoreType.DMA],
    )
    (joined,) = call(
        "join",
        join_kernel,
        [struct((2 * tokens, width // CORES), BF16)],
        [mine, hop(send, core=1)],
        [VMEM] * 2,
    )
    with jax.named_scope("panel"):
        panel_half = mirrored(joined)
    mine, send = call("norm_acts", normed_kernel, [blocks, blocks], [acts, gain], [VMEM] * 2)
    kept, kept_token = call(
        "keep",
        keep_kernel,
        [struct(parked.shape, BF16), token],
        [parked],
        [VMEM],
        [ANY, VMEM],
        [pltpu.SemaphoreType.DMA],
        after=[joined],
    )
    with jax.named_scope("weight"):
        near, middle, far, _ = gathered(weight[0], after=[joined, mine, kept_token])

    with jax.named_scope("acts"):
        forward = [mine, hop(send, core=1)]
    *pre, _ = product("forward_near", "pair", forward, near)
    pre_own, pre_other, forward_token = product(
        "forward_far", "pair", forward, middle + far, pre
    )

    backward = [panel_half, gain]
    *panel_pre, _ = product(
        "backward_near", "panel", backward, near + middle, after=[forward_token]
    )
    panel_own, panel_other, _ = product("backward_far", "panel", backward, far, panel_pre)
    with jax.named_scope("pre_acts"):
        received = hop(pre_other, core=1)
    out_rows, out_token = call(
        "out",
        out_kernel, [rows, token], [pre_own, received, acts], [VMEM] * 3
    )
    with jax.named_scope("next_acts"):
        next_acts = shifted(out_rows, 1)

    with jax.named_scope("pre"):
        received = hop(panel_other, core=1)
    with jax.named_scope("restore"):
        restored = hop(panel_half[tokens:], core=1)
    ring_blocks = (RING, CORES, BLOCK, BLOCK)
    keep, send, panel = call(
        "units",
        units_kernel,
        [struct(ring_blocks, BF16), struct(ring_blocks, BF16), rows],
        [panel_half, restored],
        [VMEM] * 2,
    )
    (delta,) = call(
        "delta", delta_kernel, [rows], [panel_own, received, grads], [VMEM] * 3, after=[keep]
    )
    with jax.named_scope("delta"):
        delta_near, delta_middle, delta_far, take_token = gathered(delta, [out_token])
    with jax.named_scope("stash"):
        stashed = mirrored(acts)

    with jax.named_scope("pair_units"):
        received = hop(send, pair=1)
    mixed, mix_token = call(
        "mix",
        mix_kernel,
        [struct((RING, PAIR, CORES, BLOCK, BLOCK), BF16), token],
        [keep, received],
        [VMEM] * 2,
    )
    units = lax.all_to_all(
        mixed,
        "dp",
        split_axis=0,
        concat_axis=0,
        tiled=True,
        axis_index_groups=[
            [(y * PAIR + x) * CORES + c for y in range(RING)] for x in range(PAIR) for c in range(CORES)
        ],
    )

    with jax.named_scope("delta_other"):
        delta_other = hop(delta, core=1)
    chunks = near + middle + far
    parts, layout = arrays_of(chunks)
    back_own, back_other = call(
        "back",
        functools.partial(back_kernel, layout),
        [back, back],
        [delta, delta_other, *parts],
        [VMEM] * (2 + len(parts)),
        scratch=[pltpu.VMEM((2 * BLOCK, width), BF16)],
        flops=2 * 2 * BLOCK * CHIPS * BLOCK * width,
    )
    with jax.named_scope("back"):
        back_received = hop(back_other, core=1)
    grad_acts, grad_token = call(
        "grads",
        grad_kernel,
        [rows, token],
        [panel, gain, grads, back_own, back_received],
        [VMEM] * 5,
        scratch=[pltpu.VMEM((tokens, width), F32)],
    )
    with jax.named_scope("next_grads"):
        next_grads = shifted(grad_acts, -1)
    *outer, near_token = product(
        "outer_near",
        "stacked",
        [units],
        delta_near + delta_middle,
        after=[grad_token],
    )
    parked_out, parked_token = call(
        "park",
        park_kernel,
        [struct(parked.shape, BF16), token],
        [park_slot, kept, stashed],
        [SMEM, ANY, VMEM],
        [ANY, VMEM],
        [pltpu.SemaphoreType.DMA],
        aliases={1: 0},
        after=[near_token],
    )

    outer_own, outer_other, outer_token = product(
        "outer_far", "stacked", [units], delta_far, outer, after=[parked_token, next_acts, next_grads]
    )
    with jax.named_scope("outer"):
        outer_received = hop(outer_other, core=1)
    next_acts, next_grads, emitted = call(
        "emit",
        emit_kernel,
        [struct((1, tokens, width), BF16), struct((1, tokens, width), BF16), token],
        [next_acts, next_grads],
        [VMEM] * 2,
        after=[outer_token],
    )
    weight_grad, gain_grad = call(
        "finish",
        finish_kernel,
        [struct((1, BLOCK, width), F32), struct((1, BLOCK), F32)],
        [outer_own, outer_received, weight, gain],
        [VMEM] * 4,
        after=[emitted],
    )
    return next_acts, next_grads, parked_out, weight_grad, gain_grad


def solution(mesh):
    return jax.shard_map(
        shards,
        mesh=mesh,
        in_specs=(
            P("section", "dp", None),
            P("section", None),
            P("section", "dp", None),
            P("section", "dp", None),
            P("section", None, "dp", None),
            P(),
            P(),
        ),
        out_specs=(
            P("section", "dp", None),
            P("section", "dp", None),
            P("section", None, "dp", None),
            P("section", "dp", None),
            P("section", "dp"),
        ),
        check_vma=False,
    )
```

```python
import functools

import jax
import jax.numpy as jnp
from jax import lax
from jax.experimental import pallas as pl
from jax.experimental.pallas import tpu as pltpu
from jax.sharding import PartitionSpec as P

EPSILON = 1e-05
RING, PAIR, CORES = 4, 2, 2
CHIPS = RING * PAIR
MEMBERS = CHIPS * CORES
BLOCK = 128
TILE = 256
MEGABYTES = 12
WIDTH = 2048

VMEM = pl.BlockSpec(memory_space=pltpu.VMEM)
SMEM = pl.BlockSpec(memory_space=pltpu.SMEM)
ANY = pl.BlockSpec(memory_space=pl.ANY)
F32, BF16 = jnp.float32, jnp.bfloat16


def struct(shape, dtype):
    return jax.ShapeDtypeStruct(shape, dtype)


def call(
    name, kernel, outs, args, specs, out_specs=None, scratch=(), flops=0, after=(), aliases=None
):
    nbytes = sum(a.size * a.dtype.itemsize for a in list(args) + list(outs))
    given = len(args)

    def body(*refs):
        kernel(*refs[:given], *refs[given + len(after) :])

    return pl.pallas_call(
        body,
        out_shape=list(outs),
        in_specs=list(specs) + [ANY] * len(after),
        out_specs=list(out_specs) if out_specs else [VMEM] * len(outs),
        scratch_shapes=list(scratch),
        input_output_aliases=aliases or {},
        name=name,
        cost_estimate=pl.CostEstimate(flops=flops, bytes_accessed=nbytes, transcendentals=0),
        compiler_params=pltpu.CompilerParams(vmem_limit_bytes=MEGABYTES * 1024 * 1024),
    )(*args, *after)


def mirrored(block):
    count = lax.axis_size("section")
    return lax.ppermute(block, "section", [(i, count - 1 - i) for i in range(count)])


def shifted(block, distance):
    count = lax.axis_size("section")
    return lax.ppermute(block, "section", [((i - distance) % count, i) for i in range(count)])


def hop(block, ring=0, pair=0, core=0):
    route = []
    for i in range(MEMBERS):
        y, x, c = i // (PAIR * CORES), i // CORES % PAIR, i % CORES
        route.append((i, (((y + ring) % RING) * PAIR + (x ^ pair)) * CORES + (c ^ core)))
    return lax.ppermute(block, "dp", route)


def gathered(own, after=(), take_after=()):
    rows, width = own.shape
    half = rows // 2
    with jax.named_scope("below"):
        below = hop(own, ring=1)
    with jax.named_scope("above"):
        above = hop(own, ring=-1)
    with jax.named_scope("pair"):
        pair = hop(own, pair=1)
    packed = struct((half + rows, width), own.dtype)
    up, down = call(
        "pack",
        pack_kernel,
        [packed, packed],
        [below, above, pair],
        [VMEM] * 3,
        scratch=[pltpu.SemaphoreType.DMA((4,))],
        after=after,
    )
    with jax.named_scope("up"):
        up = hop(up, ring=1)
    with jax.named_scope("down"):
        down = hop(down, ring=-1)
    halves = struct((half, width), own.dtype)
    low, high, token = call(
        "take",
        take_kernel,
        [halves, halves, struct((8, BLOCK), F32)],
        [up, down],
        [VMEM] * 2,
        scratch=[pltpu.SemaphoreType.DMA((2,))],
        after=take_after,
    )
    with jax.named_scope("far_up"):
        far_up = hop(low, ring=1)
    with jax.named_scope("far_down"):
        far_down = hop(high, ring=-1)
    near = [
        (0, 0, [(own, 0, rows)]),
        (-1, 0, [(below, 0, rows)]),
        (1, 0, [(above, 0, rows)]),
        (0, 1, [(pair, 0, rows)]),
    ]
    middle = [
        (2, 0, [(up, 0, half), (down, rows, rows + half)]),
        (-1, 1, [(up, half, half + rows)]),
        (1, 1, [(down, 0, rows)]),
    ]
    far = [(2, 1, [(far_up, 0, half), (far_down, 0, half)])]
    return near, middle, far, token


def arrays_of(chunks):
    arrays, layout = [], []
    for up, other, pieces in chunks:
        placed = []
        for array, first, last in pieces:
            at = next((i for i, a in enumerate(arrays) if a is array), len(arrays))
            if at == len(arrays):
                arrays.append(array)
            placed.append((at, first, last))
        layout.append((up, other, placed))
    return arrays, layout


def place():
    member = lax.axis_index("dp")
    core = lax.rem(member, CORES)
    return member, core


def chip_of(up, other):
    member = lax.axis_index("dp")
    ring_at = lax.div(member, PAIR * CORES)
    pair_at = lax.rem(lax.div(member, CORES), PAIR)
    pair_to = 1 - pair_at if other else pair_at
    return lax.rem(ring_at + up + RING, RING) * PAIR + pair_to


def columns_of(step):
    return pl.ds(pl.multiple_of(step * TILE, TILE), TILE)


def inverse_rms(values):
    return lax.rsqrt(jnp.mean(values * values, -1, keepdims=True) + EPSILON)


def split_kernel(slots, held, mine, send, panel, sem):
    _, core = place()
    partner = lax.axis_size("section") - 1 - lax.axis_index("section")
    copy = pltpu.make_async_copy(held.at[0, slots[partner]], panel, sem)
    copy.start()
    copy.wait()
    for chip in range(CHIPS):
        at, to = chip * CORES * BLOCK, chip * BLOCK
        first, second = panel[:, at : at + BLOCK], panel[:, at + BLOCK : at + 2 * BLOCK]
        mine[:, to : to + BLOCK] = jnp.where(core == 0, first, second)
        send[:, to : to + BLOCK] = jnp.where(core == 0, second, first)


def join_kernel(mine, received, joined):
    rows = mine.shape[0]
    joined[:rows] = mine[...]
    joined[rows:] = received[...]


def copy_all(pairs, sems):
    copies = [pltpu.make_async_copy(a, b, sems.at[i]) for i, (a, b) in enumerate(pairs)]
    for copy in copies:
        copy.start()
    return copies


def pack_kernel(below, above, pair, up, down, sems):
    rows = pair.shape[0]
    half = rows // 2
    copies = copy_all(
        [
            (pair, up.at[pl.ds(half, rows)]),
            (pair, down.at[pl.ds(0, rows)]),
            (below.at[pl.ds(0, half)], up.at[pl.ds(0, half)]),
            (above.at[pl.ds(half, half)], down.at[pl.ds(rows, half)]),
        ],
        sems,
    )
    for copy in copies:
        copy.wait()


def take_kernel(up, down, low, high, token, sems):
    token[...] = jnp.zeros_like(token)
    rows = low.shape[0]
    copies = copy_all([(up.at[pl.ds(rows, rows)], low), (down.at[pl.ds(rows, rows)], high)], sems)
    for copy in copies:
        copy.wait()


def units_kernel(half, received, keep, send, panel):
    member, core = place()
    pair_at = lax.rem(lax.div(member, CORES), PAIR)
    rows = received.shape[0]
    for chip in range(CHIPS):
        at, of = chip * CORES * BLOCK, chip * BLOCK
        own, other = half[:rows, of : of + BLOCK], received[:, of : of + BLOCK]
        panel[:, at : at + BLOCK] = jnp.where(core == 0, own, other)
        panel[:, at + BLOCK : at + 2 * BLOCK] = jnp.where(core == 0, other, own)
    values = panel[...].astype(F32)
    unit = values * inverse_rms(values)
    for y in range(RING):
        blocks = []
        for block in range(PAIR * CORES):
            at = (y * PAIR * CORES + block) * BLOCK
            blocks.append(jnp.transpose(unit[:, at : at + BLOCK]).astype(BF16))
        for c in range(CORES):
            mine = [jnp.where(core == 0, blocks[x + c], blocks[x + 1 - c]) for x in (0, CORES)]
            keep[y, c] = jnp.where(pair_at == 0, mine[0], mine[1])
            send[y, c] = jnp.where(pair_at == 0, mine[1], mine[0])


def mix_kernel(keep, received, mixed, token):
    token[...] = jnp.zeros_like(token)
    for y in range(RING):
        mixed[y, 0] = keep[y]
        mixed[y, 1] = received[y]


def normed_kernel(rows, gain, mine, send):
    _, core = place()
    values = rows[...].astype(F32)
    unit = values * inverse_rms(values)
    normed = (unit * gain[...]).astype(BF16)
    for chip in range(CHIPS):
        at = chip * CORES * BLOCK
        first, second = normed[:, at : at + BLOCK], normed[:, at + BLOCK : at + 2 * BLOCK]
        mine[chip] = jnp.where(core == 0, first, second)
        send[chip] = jnp.where(core == 0, second, first)


def product_kernel(layout, kind, added, *refs):
    refs = list(refs)
    left, token = refs.pop(), refs.pop(-1)
    token[...] = jnp.zeros_like(token)
    out_own, out_other = refs[-2:]
    del refs[-2:]
    _, core = place()
    first_ref, second_ref = refs.pop(0), None if kind == "stacked" else refs.pop(0)
    totals = [refs.pop(), refs.pop()][::-1] if added else None
    for k, (up, to_other, _) in enumerate(layout):
        chip = chip_of(up, to_other)
        columns = slice(k * BLOCK, (k + 1) * BLOCK)
        if kind == "stacked":
            left[:BLOCK, columns] = first_ref[lax.div(chip, PAIR), to_other, 0]
            left[BLOCK:, columns] = first_ref[lax.div(chip, PAIR), to_other, 1]
        elif kind == "pair":
            left[:BLOCK, columns] = first_ref[chip]
            left[BLOCK:, columns] = second_ref[chip]
        else:
            at = pl.ds(pl.multiple_of(chip * BLOCK, BLOCK), BLOCK)
            of = pl.ds(pl.multiple_of((chip * CORES + core) * BLOCK, BLOCK), BLOCK)
            left[:, columns] = (first_ref[:, at].astype(F32) * second_ref[:, of]).astype(BF16)

    @pl.loop(0, WIDTH // TILE)
    def _(step):
        columns = columns_of(step)
        right = jnp.concatenate(
            [refs[i][first:last, columns] for _, _, placed in layout for i, first, last in placed], 0
        )
        result = jnp.dot(left[...], right, preferred_element_type=F32)
        low, high = result[:BLOCK], result[BLOCK:]
        if added:
            low, high = low + totals[0][:, columns], high + totals[1][:, columns]
        out_own[:, columns] = low
        out_other[:, columns] = high.astype(out_other.dtype)

    if kind == "panel":
        values = first_ref[...].astype(F32)
        squares = jnp.broadcast_to(jnp.sum(values * values, -1, keepdims=True), (2 * BLOCK, BLOCK))
        out_own[:, WIDTH:] = squares[:BLOCK]
        rounded = squares[BLOCK:].astype(BF16)
        out_other[:, WIDTH : WIDTH + BLOCK] = rounded
        out_other[:, WIDTH + BLOCK :] = (squares[BLOCK:] - rounded.astype(F32)).astype(BF16)


def product(name, kind, blocks, chunks, totals=(), after=()):
    parts, layout = arrays_of(chunks)
    depth, width = len(chunks) * BLOCK, WIDTH + (BLOCK if kind == "panel" else 0)
    last = struct((BLOCK, width + (BLOCK if kind == "panel" else 0)), BF16)
    args = [*blocks, *parts, *totals]
    out = struct((BLOCK, width), F32)
    return call(
        name,
        functools.partial(product_kernel, layout, kind, bool(totals)),
        [out, last if totals or kind == "panel" else out, struct((8, BLOCK), F32)],
        args,
        [VMEM] * len(args),
        scratch=[pltpu.VMEM((2 * BLOCK, depth), BF16)],
        flops=2 * 2 * BLOCK * depth * width,
        after=after,
    )


def delta_kernel(own, received, grads, delta):
    squares = own[:, WIDTH : WIDTH + 1] + (
        received[:, WIDTH : WIDTH + 1].astype(F32)
        + received[:, WIDTH + BLOCK : WIDTH + BLOCK + 1].astype(F32)
    )
    inverse = lax.rsqrt(squares * (1.0 / WIDTH) + EPSILON)

    @pl.loop(0, WIDTH // TILE)
    def _(step):
        columns = columns_of(step)
        pre_act = (own[:, columns] + received[:, columns].astype(F32)) * inverse
        sigma = jax.nn.sigmoid(pre_act)
        grad_f = grads[:, columns].astype(F32)
        delta[:, columns] = (grad_f * sigma * (1.0 + pre_act * (1.0 - sigma))).astype(BF16)


def out_kernel(own, received, acts, out, token):
    token[...] = jnp.zeros_like(token)

    @pl.loop(0, out.shape[1] // TILE)
    def _(step):
        columns = columns_of(step)
        pre_act = own[:, columns] + received[:, columns].astype(F32)
        values = acts[:, columns].astype(F32)
        out[:, columns] = (values + pre_act * jax.nn.sigmoid(pre_act)).astype(BF16)


def back_kernel(layout, delta_own, delta_other, *refs):
    refs = list(refs)
    left = refs.pop()
    back_own, back_other = refs[-2:]
    left[:BLOCK] = delta_own[...]
    left[BLOCK:] = delta_other[...]
    for k in range(0, len(layout), 2):
        right = jnp.concatenate(
            [refs[i][first:last] for _, _, placed in layout[k : k + 2] for i, first, last in placed], 0
        )
        result = lax.dot_general(
            left[...], right, (((1,), (1,)), ((), ())), preferred_element_type=F32
        )
        for i, (up, other, _) in enumerate(layout[k : k + 2]):
            chip = chip_of(up, other)
            back_own[chip] = result[:BLOCK, i * BLOCK : (i + 1) * BLOCK]
            back_other[chip] = result[BLOCK:, i * BLOCK : (i + 1) * BLOCK]


def grad_kernel(panel, gain, grads, back_own, back_received, grad_acts, token, through):
    token[...] = jnp.zeros_like(token)
    _, core = place()
    values = panel[...].astype(F32)
    inverse = inverse_rms(values)
    for chip in range(CHIPS):
        at = chip * CORES * BLOCK
        own, received = back_own[chip], back_received[chip]
        through[:, at : at + BLOCK] = jnp.where(core == 0, own, received)
        through[:, at + BLOCK : at + 2 * BLOCK] = jnp.where(core == 0, received, own)
    unit = values * inverse
    scaled = through[...] * gain[...]
    mean = jnp.mean(scaled * unit, -1, keepdims=True)
    grad_acts[...] = (grads[...].astype(F32) + inverse * (scaled - unit * mean)).astype(BF16)


def keep_kernel(held, out, token, sem):
    copy = pltpu.make_async_copy(held, out, sem)
    copy.start()
    token[...] = jnp.zeros_like(token)
    copy.wait()


def park_kernel(slots, kept, stashed, out, token, sem):
    del kept
    partner = lax.axis_size("section") - 1 - lax.axis_index("section")
    copy = pltpu.make_async_copy(stashed, out.at[0, slots[partner]], sem)
    copy.start()
    token[...] = jnp.zeros_like(token)
    copy.wait()


def emit_kernel(acts, grads, next_acts, next_grads, token):
    next_acts[0] = acts[...]
    next_grads[0] = grads[...]
    token[...] = jnp.zeros_like(token)


def finish_kernel(own, received, weight, gain, weight_grad, gain_grad):
    member, _ = place()
    own_gain = gain[:, pl.ds(pl.multiple_of(member * BLOCK, BLOCK), BLOCK)]
    scale = jnp.transpose(jnp.broadcast_to(own_gain, (BLOCK, BLOCK)))[:, :1]
    total = jnp.zeros((BLOCK, 1), F32)
    for at in range(0, own.shape[1], TILE):
        outer = own[:, at : at + TILE] + received[:, at : at + TILE].astype(F32)
        weight_grad[0, :, at : at + TILE] = outer * scale
        total += jnp.sum(outer * weight[0, :, at : at + TILE].astype(F32), -1, keepdims=True)
    gain_grad[...] = jnp.transpose(jnp.broadcast_to(total, (BLOCK, BLOCK)))[:1]


def shards(weight, gain, acts_in, grads_in, parked, fetch_slot, park_slot):
    tokens, width = acts_in.shape[1:]
    acts, grads = acts_in[0], grads_in[0]
    rows, blocks = struct((tokens, width), BF16), struct((CHIPS, BLOCK, BLOCK), BF16)
    token = struct((8, BLOCK), F32)
    back = struct((CHIPS, BLOCK, BLOCK), F32)

    half = struct((tokens, width // CORES), BF16)
    mine, send = call(
        "split",
        split_kernel,
        [half, half],
        [fetch_slot, parked],
        [SMEM, ANY],
        scratch=[pltpu.VMEM((tokens, width), BF16), pltpu.SemaphoreType.DMA],
    )
    (joined,) = call(
        "join",
        join_kernel,
        [struct((2 * tokens, width // CORES), BF16)],
        [mine, hop(send, core=1)],
        [VMEM] * 2,
    )
    with jax.named_scope("panel"):
        panel_half = mirrored(joined)
    mine, send = call("norm_acts", normed_kernel, [blocks, blocks], [acts, gain], [VMEM] * 2)
    kept, kept_token = call(
        "keep",
        keep_kernel,
        [struct(parked.shape, BF16), token],
        [parked],
        [VMEM],
        [ANY, VMEM],
        [pltpu.SemaphoreType.DMA],
        after=[joined],
    )
    with jax.named_scope("weight"):
        near, middle, far, _ = gathered(weight[0], after=[joined, mine, kept_token])

    with jax.named_scope("acts"):
        forward = [mine, hop(send, core=1)]
    *pre, _ = product("forward_near", "pair", forward, near)
    pre_own, pre_other, forward_token = product(
        "forward_far", "pair", forward, middle + far, pre
    )

    backward = [panel_half, gain]
    panel_own, panel_other, _ = product(
        "backward", "panel", backward, near + middle + far, after=[forward_token]
    )
    with jax.named_scope("pre_acts"):
        received = hop(pre_other, core=1)
    out_rows, out_token = call(
        "out",
        out_kernel, [rows, token], [pre_own, received, acts], [VMEM] * 3
    )
    with jax.named_scope("next_acts"):
        next_acts = shifted(out_rows, 1)

    with jax.named_scope("pre"):
        received = hop(panel_other, core=1)
    with jax.named_scope("restore"):
        restored = hop(panel_half[tokens:], core=1)
    ring_blocks = (RING, CORES, BLOCK, BLOCK)
    keep, send, panel = call(
        "units",
        units_kernel,
        [struct(ring_blocks, BF16), struct(ring_blocks, BF16), rows],
        [panel_half, restored],
        [VMEM] * 2,
    )
    (delta,) = call(
        "delta", delta_kernel, [rows], [panel_own, received, grads], [VMEM] * 3, after=[keep]
    )
    with jax.named_scope("delta"):
        delta_near, delta_middle, delta_far, take_token = gathered(delta, [out_token])
    with jax.named_scope("stash"):
        stashed = mirrored(acts)

    with jax.named_scope("pair_units"):
        received = hop(send, pair=1)
    mixed, mix_token = call(
        "mix",
        mix_kernel,
        [struct((RING, PAIR, CORES, BLOCK, BLOCK), BF16), token],
        [keep, received],
        [VMEM] * 2,
    )
    units = lax.all_to_all(
        mixed,
        "dp",
        split_axis=0,
        concat_axis=0,
        tiled=True,
        axis_index_groups=[
            [(y * PAIR + x) * CORES + c for y in range(RING)] for x in range(PAIR) for c in range(CORES)
        ],
    )

    with jax.named_scope("delta_other"):
        delta_other = hop(delta, core=1)
    chunks = near + middle + far
    parts, layout = arrays_of(chunks)
    back_own, back_other = call(
        "back",
        functools.partial(back_kernel, layout),
        [back, back],
        [delta, delta_other, *parts],
        [VMEM] * (2 + len(parts)),
        scratch=[pltpu.VMEM((2 * BLOCK, width), BF16)],
        flops=2 * 2 * BLOCK * CHIPS * BLOCK * width,
    )
    with jax.named_scope("back"):
        back_received = hop(back_other, core=1)
    grad_acts, grad_token = call(
        "grads",
        grad_kernel,
        [rows, token],
        [panel, gain, grads, back_own, back_received],
        [VMEM] * 5,
        scratch=[pltpu.VMEM((tokens, width), F32)],
    )
    with jax.named_scope("next_grads"):
        next_grads = shifted(grad_acts, -1)
    *outer, near_token = product(
        "outer_near",
        "stacked",
        [units],
        delta_near + delta_middle,
        after=[grad_token],
    )
    parked_out, parked_token = call(
        "park",
        park_kernel,
        [struct(parked.shape, BF16), token],
        [park_slot, kept, stashed],
        [SMEM, ANY, VMEM],
        [ANY, VMEM],
        [pltpu.SemaphoreType.DMA],
        aliases={1: 0},
        after=[near_token],
    )

    outer_own, outer_other, outer_token = product(
        "outer_far", "stacked", [units], delta_far, outer, after=[parked_token, next_acts, next_grads]
    )
    with jax.named_scope("outer"):
        outer_received = hop(outer_other, core=1)
    next_acts, next_grads, emitted = call(
        "emit",
        emit_kernel,
        [struct((1, tokens, width), BF16), struct((1, tokens, width), BF16), token],
        [next_acts, next_grads],
        [VMEM] * 2,
        after=[outer_token],
    )
    weight_grad, gain_grad = call(
        "finish",
        finish_kernel,
        [struct((1, BLOCK, width), F32), struct((1, BLOCK), F32)],
        [outer_own, outer_received, weight, gain],
        [VMEM] * 4,
        after=[emitted],
    )
    return next_acts, next_grads, parked_out, weight_grad, gain_grad


def solution(mesh):
    return jax.shard_map(
        shards,
        mesh=mesh,
        in_specs=(
            P("section", "dp", None),
            P("section", None),
            P("section", "dp", None),
            P("section", "dp", None),
            P("section", None, "dp", None),
            P(),
            P(),
        ),
        out_specs=(
            P("section", "dp", None),
            P("section", "dp", None),
            P("section", None, "dp", None),
            P("section", "dp", None),
            P("section", "dp"),
        ),
        check_vma=False,
    )
```

```python
import functools

import jax
import jax.numpy as jnp
from jax import lax
from jax.experimental import pallas as pl
from jax.experimental.pallas import tpu as pltpu
from jax.sharding import PartitionSpec as P

EPSILON = 1e-05
RING, PAIR, CORES = 4, 2, 2
CHIPS = RING * PAIR
MEMBERS = CHIPS * CORES
BLOCK = 128
TILE = 1024
MEGABYTES = 12
WIDTH = 2048

VMEM = pl.BlockSpec(memory_space=pltpu.VMEM)
SMEM = pl.BlockSpec(memory_space=pltpu.SMEM)
ANY = pl.BlockSpec(memory_space=pl.ANY)
F32, BF16 = jnp.float32, jnp.bfloat16


def struct(shape, dtype):
    return jax.ShapeDtypeStruct(shape, dtype)


def call(
    name, kernel, outs, args, specs, out_specs=None, scratch=(), flops=0, after=(), aliases=None
):
    nbytes = sum(a.size * a.dtype.itemsize for a in list(args) + list(outs))
    given = len(args)

    def body(*refs):
        kernel(*refs[:given], *refs[given + len(after) :])

    return pl.pallas_call(
        body,
        out_shape=list(outs),
        in_specs=list(specs) + [ANY] * len(after),
        out_specs=list(out_specs) if out_specs else [VMEM] * len(outs),
        scratch_shapes=list(scratch),
        input_output_aliases=aliases or {},
        name=name,
        cost_estimate=pl.CostEstimate(flops=flops, bytes_accessed=nbytes, transcendentals=0),
        compiler_params=pltpu.CompilerParams(vmem_limit_bytes=MEGABYTES * 1024 * 1024),
    )(*args, *after)


def mirrored(block):
    count = lax.axis_size("section")
    return lax.ppermute(block, "section", [(i, count - 1 - i) for i in range(count)])


def shifted(block, distance):
    count = lax.axis_size("section")
    return lax.ppermute(block, "section", [((i - distance) % count, i) for i in range(count)])


def hop(block, ring=0, pair=0, core=0):
    route = []
    for i in range(MEMBERS):
        y, x, c = i // (PAIR * CORES), i // CORES % PAIR, i % CORES
        route.append((i, (((y + ring) % RING) * PAIR + (x ^ pair)) * CORES + (c ^ core)))
    return lax.ppermute(block, "dp", route)


def gathered(own, after=(), take_after=()):
    rows, width = own.shape
    half = rows // 2
    with jax.named_scope("below"):
        below = hop(own, ring=1)
    with jax.named_scope("above"):
        above = hop(own, ring=-1)
    with jax.named_scope("pair"):
        pair = hop(own, pair=1)
    packed = struct((half + rows, width), own.dtype)
    up, down = call(
        "pack",
        pack_kernel,
        [packed, packed],
        [below, above, pair],
        [VMEM] * 3,
        scratch=[pltpu.SemaphoreType.DMA((4,))],
        after=after,
    )
    with jax.named_scope("up"):
        up = hop(up, ring=1)
    with jax.named_scope("down"):
        down = hop(down, ring=-1)
    halves = struct((half, width), own.dtype)
    low, high, token = call(
        "take",
        take_kernel,
        [halves, halves, struct((8, BLOCK), F32)],
        [up, down],
        [VMEM] * 2,
        scratch=[pltpu.SemaphoreType.DMA((2,))],
        after=take_after,
    )
    with jax.named_scope("far_up"):
        far_up = hop(low, ring=1)
    with jax.named_scope("far_down"):
        far_down = hop(high, ring=-1)
    near = [
        (0, 0, [(own, 0, rows)]),
        (-1, 0, [(below, 0, rows)]),
        (1, 0, [(above, 0, rows)]),
        (0, 1, [(pair, 0, rows)]),
    ]
    middle = [
        (2, 0, [(up, 0, half), (down, rows, rows + half)]),
        (-1, 1, [(up, half, half + rows)]),
        (1, 1, [(down, 0, rows)]),
    ]
    far = [(2, 1, [(far_up, 0, half), (far_down, 0, half)])]
    return near, middle, far, token


def arrays_of(chunks):
    arrays, layout = [], []
    for up, other, pieces in chunks:
        placed = []
        for array, first, last in pieces:
            at = next((i for i, a in enumerate(arrays) if a is array), len(arrays))
            if at == len(arrays):
                arrays.append(array)
            placed.append((at, first, last))
        layout.append((up, other, placed))
    return arrays, layout


def place():
    member = lax.axis_index("dp")
    core = lax.rem(member, CORES)
    return member, core


def chip_of(up, other):
    member = lax.axis_index("dp")
    ring_at = lax.div(member, PAIR * CORES)
    pair_at = lax.rem(lax.div(member, CORES), PAIR)
    pair_to = 1 - pair_at if other else pair_at
    return lax.rem(ring_at + up + RING, RING) * PAIR + pair_to


def columns_of(step):
    return pl.ds(pl.multiple_of(step * TILE, TILE), TILE)


def inverse_rms(values):
    return lax.rsqrt(jnp.mean(values * values, -1, keepdims=True) + EPSILON)


def split_kernel(slots, held, mine, send, panel, sem):
    _, core = place()
    partner = lax.axis_size("section") - 1 - lax.axis_index("section")
    copy = pltpu.make_async_copy(held.at[0, slots[partner]], panel, sem)
    copy.start()
    copy.wait()
    for chip in range(CHIPS):
        at, to = chip * CORES * BLOCK, chip * BLOCK
        first, second = panel[:, at : at + BLOCK], panel[:, at + BLOCK : at + 2 * BLOCK]
        mine[:, to : to + BLOCK] = jnp.where(core == 0, first, second)
        send[:, to : to + BLOCK] = jnp.where(core == 0, second, first)


def join_kernel(mine, received, joined):
    rows = mine.shape[0]
    joined[:rows] = mine[...]
    joined[rows:] = received[...]


def copy_all(pairs, sems):
    copies = [pltpu.make_async_copy(a, b, sems.at[i]) for i, (a, b) in enumerate(pairs)]
    for copy in copies:
        copy.start()
    return copies


def pack_kernel(below, above, pair, up, down, sems):
    rows = pair.shape[0]
    half = rows // 2
    copies = copy_all(
        [
            (pair, up.at[pl.ds(half, rows)]),
            (pair, down.at[pl.ds(0, rows)]),
            (below.at[pl.ds(0, half)], up.at[pl.ds(0, half)]),
            (above.at[pl.ds(half, half)], down.at[pl.ds(rows, half)]),
        ],
        sems,
    )
    for copy in copies:
        copy.wait()


def take_kernel(up, down, low, high, token, sems):
    token[...] = jnp.zeros_like(token)
    rows = low.shape[0]
    copies = copy_all([(up.at[pl.ds(rows, rows)], low), (down.at[pl.ds(rows, rows)], high)], sems)
    for copy in copies:
        copy.wait()


def units_kernel(half, received, grads, keep, send, panel, grads_here):
    member, core = place()
    pair_at = lax.rem(lax.div(member, CORES), PAIR)
    grads_here[...] = grads[...]
    rows = received.shape[0]
    for chip in range(CHIPS):
        at, of = chip * CORES * BLOCK, chip * BLOCK
        own, other = half[:rows, of : of + BLOCK], received[:, of : of + BLOCK]
        panel[:, at : at + BLOCK] = jnp.where(core == 0, own, other)
        panel[:, at + BLOCK : at + 2 * BLOCK] = jnp.where(core == 0, other, own)
    values = panel[...].astype(F32)
    unit = values * inverse_rms(values)
    for y in range(RING):
        blocks = []
        for block in range(PAIR * CORES):
            at = (y * PAIR * CORES + block) * BLOCK
            blocks.append(jnp.transpose(unit[:, at : at + BLOCK]).astype(BF16))
        for c in range(CORES):
            mine = [jnp.where(core == 0, blocks[x + c], blocks[x + 1 - c]) for x in (0, CORES)]
            keep[y, c] = jnp.where(pair_at == 0, mine[0], mine[1])
            send[y, c] = jnp.where(pair_at == 0, mine[1], mine[0])


def mix_kernel(keep, received, mixed, token):
    token[...] = jnp.zeros_like(token)
    for y in range(RING):
        mixed[y, 0] = keep[y]
        mixed[y, 1] = received[y]


def normed_kernel(rows, gain, mine, send):
    _, core = place()
    values = rows[...].astype(F32)
    unit = values * inverse_rms(values)
    normed = (unit * gain[...]).astype(BF16)
    for chip in range(CHIPS):
        at = chip * CORES * BLOCK
        first, second = normed[:, at : at + BLOCK], normed[:, at + BLOCK : at + 2 * BLOCK]
        mine[chip] = jnp.where(core == 0, first, second)
        send[chip] = jnp.where(core == 0, second, first)


def product_kernel(layout, kind, added, *refs):
    refs = list(refs)
    left, token = refs.pop(), refs.pop(-1)
    token[...] = jnp.zeros_like(token)
    out_own, out_other = refs[-2:]
    del refs[-2:]
    _, core = place()
    first_ref, second_ref = refs.pop(0), None if kind == "stacked" else refs.pop(0)
    totals = [refs.pop(), refs.pop()][::-1] if added else None
    for k, (up, to_other, _) in enumerate(layout):
        chip = chip_of(up, to_other)
        columns = slice(k * BLOCK, (k + 1) * BLOCK)
        if kind == "stacked":
            left[:BLOCK, columns] = first_ref[lax.div(chip, PAIR), to_other, 0]
            left[BLOCK:, columns] = first_ref[lax.div(chip, PAIR), to_other, 1]
        elif kind == "pair":
            left[:BLOCK, columns] = first_ref[chip]
            left[BLOCK:, columns] = second_ref[chip]
        else:
            at = pl.ds(pl.multiple_of(chip * BLOCK, BLOCK), BLOCK)
            of = pl.ds(pl.multiple_of((chip * CORES + core) * BLOCK, BLOCK), BLOCK)
            left[:, columns] = (first_ref[:, at].astype(F32) * second_ref[:, of]).astype(BF16)

    @pl.loop(0, WIDTH // TILE)
    def _(step):
        columns = columns_of(step)
        right = jnp.concatenate(
            [refs[i][first:last, columns] for _, _, placed in layout for i, first, last in placed], 0
        )
        result = jnp.dot(left[...], right, preferred_element_type=F32)
        low, high = result[:BLOCK], result[BLOCK:]
        if added:
            low, high = low + totals[0][:, columns], high + totals[1][:, columns]
        out_own[:, columns] = low
        out_other[:, columns] = high.astype(out_other.dtype)

    if kind == "panel":
        values = first_ref[...].astype(F32)
        squares = jnp.broadcast_to(jnp.sum(values * values, -1, keepdims=True), (2 * BLOCK, BLOCK))
        out_own[:, WIDTH:] = squares[:BLOCK]
        rounded = squares[BLOCK:].astype(BF16)
        out_other[:, WIDTH : WIDTH + BLOCK] = rounded
        out_other[:, WIDTH + BLOCK :] = (squares[BLOCK:] - rounded.astype(F32)).astype(BF16)


def product(name, kind, blocks, chunks, totals=(), after=()):
    parts, layout = arrays_of(chunks)
    depth, width = len(chunks) * BLOCK, WIDTH + (BLOCK if kind == "panel" else 0)
    last = struct((BLOCK, width + (BLOCK if kind == "panel" else 0)), BF16)
    args = [*blocks, *parts, *totals]
    out = struct((BLOCK, width), F32)
    return call(
        name,
        functools.partial(product_kernel, layout, kind, bool(totals)),
        [out, last if totals or kind == "panel" else out, struct((8, BLOCK), F32)],
        args,
        [VMEM] * len(args),
        scratch=[pltpu.VMEM((2 * BLOCK, depth), BF16)],
        flops=2 * 2 * BLOCK * depth * width,
        after=after,
    )


def delta_kernel(own, received, grads, delta):
    squares = own[:, WIDTH : WIDTH + 1] + (
        received[:, WIDTH : WIDTH + 1].astype(F32)
        + received[:, WIDTH + BLOCK : WIDTH + BLOCK + 1].astype(F32)
    )
    inverse = lax.rsqrt(squares * (1.0 / WIDTH) + EPSILON)

    @pl.loop(0, WIDTH // TILE)
    def _(step):
        columns = columns_of(step)
        pre_act = (own[:, columns] + received[:, columns].astype(F32)) * inverse
        sigma = jax.nn.sigmoid(pre_act)
        grad_f = grads[:, columns].astype(F32)
        delta[:, columns] = (grad_f * sigma * (1.0 + pre_act * (1.0 - sigma))).astype(BF16)


def out_kernel(own, received, acts, out, token):
    token[...] = jnp.zeros_like(token)

    @pl.loop(0, out.shape[1] // TILE)
    def _(step):
        columns = columns_of(step)
        pre_act = own[:, columns] + received[:, columns].astype(F32)
        values = acts[:, columns].astype(F32)
        out[:, columns] = (values + pre_act * jax.nn.sigmoid(pre_act)).astype(BF16)


def back_kernel(layout, delta_own, delta_other, *refs):
    refs = list(refs)
    left = refs.pop()
    back_own, back_other = refs[-2:]
    left[:BLOCK] = delta_own[...]
    left[BLOCK:] = delta_other[...]
    for k in range(0, len(layout), 2):
        right = jnp.concatenate(
            [refs[i][first:last] for _, _, placed in layout[k : k + 2] for i, first, last in placed], 0
        )
        result = lax.dot_general(
            left[...], right, (((1,), (1,)), ((), ())), preferred_element_type=F32
        )
        for i, (up, other, _) in enumerate(layout[k : k + 2]):
            chip = chip_of(up, other)
            back_own[chip] = result[:BLOCK, i * BLOCK : (i + 1) * BLOCK]
            back_other[chip] = result[BLOCK:, i * BLOCK : (i + 1) * BLOCK]


def grad_kernel(panel, gain, grads, back_own, back_received, grad_acts, token, through):
    token[...] = jnp.zeros_like(token)
    _, core = place()
    values = panel[...].astype(F32)
    inverse = inverse_rms(values)
    for chip in range(CHIPS):
        at = chip * CORES * BLOCK
        own, received = back_own[chip], back_received[chip]
        through[:, at : at + BLOCK] = jnp.where(core == 0, own, received)
        through[:, at + BLOCK : at + 2 * BLOCK] = jnp.where(core == 0, received, own)
    unit = values * inverse
    scaled = through[...] * gain[...]
    mean = jnp.mean(scaled * unit, -1, keepdims=True)
    grad_acts[...] = (grads[...].astype(F32) + inverse * (scaled - unit * mean)).astype(BF16)


def keep_kernel(held, out, token, sem):
    copy = pltpu.make_async_copy(held, out, sem)
    copy.start()
    token[...] = jnp.zeros_like(token)
    copy.wait()


def park_kernel(slots, kept, stashed, out, token, sem):
    del kept
    partner = lax.axis_size("section") - 1 - lax.axis_index("section")
    copy = pltpu.make_async_copy(stashed, out.at[0, slots[partner]], sem)
    copy.start()
    token[...] = jnp.zeros_like(token)
    copy.wait()


def emit_kernel(acts, grads, next_acts, next_grads, token):
    next_acts[0] = acts[...]
    next_grads[0] = grads[...]
    token[...] = jnp.zeros_like(token)


def finish_kernel(own, received, weight, gain, weight_grad, gain_grad):
    member, _ = place()
    own_gain = gain[:, pl.ds(pl.multiple_of(member * BLOCK, BLOCK), BLOCK)]
    scale = jnp.transpose(jnp.broadcast_to(own_gain, (BLOCK, BLOCK)))[:, :1]
    total = jnp.zeros((BLOCK, 1), F32)
    for at in range(0, own.shape[1], TILE):
        outer = own[:, at : at + TILE] + received[:, at : at + TILE].astype(F32)
        weight_grad[0, :, at : at + TILE] = outer * scale
        total += jnp.sum(outer * weight[0, :, at : at + TILE].astype(F32), -1, keepdims=True)
    gain_grad[...] = jnp.transpose(jnp.broadcast_to(total, (BLOCK, BLOCK)))[:1]


def shards(weight, gain, acts_in, grads_in, parked, fetch_slot, park_slot):
    tokens, width = acts_in.shape[1:]
    acts, grads = acts_in[0], grads_in[0]
    rows, blocks = struct((tokens, width), BF16), struct((CHIPS, BLOCK, BLOCK), BF16)
    token = struct((8, BLOCK), F32)
    back = struct((CHIPS, BLOCK, BLOCK), F32)

    half = struct((tokens, width // CORES), BF16)
    mine, send = call(
        "split",
        split_kernel,
        [half, half],
        [fetch_slot, parked],
        [SMEM, ANY],
        scratch=[pltpu.VMEM((tokens, width), BF16), pltpu.SemaphoreType.DMA],
    )
    (joined,) = call(
        "join",
        join_kernel,
        [struct((2 * tokens, width // CORES), BF16)],
        [mine, hop(send, core=1)],
        [VMEM] * 2,
    )
    with jax.named_scope("panel"):
        panel_half = mirrored(joined)
    mine, send = call("norm_acts", normed_kernel, [blocks, blocks], [acts, gain], [VMEM] * 2)
    kept, kept_token = call(
        "keep",
        keep_kernel,
        [struct(parked.shape, BF16), token],
        [parked],
        [VMEM],
        [ANY, VMEM],
        [pltpu.SemaphoreType.DMA],
        after=[joined],
    )
    with jax.named_scope("weight"):
        near, middle, far, _ = gathered(weight[0], after=[joined, mine, kept_token])

    with jax.named_scope("acts"):
        forward = [mine, hop(send, core=1)]
    *pre, _ = product("forward_near", "pair", forward, near)
    pre_own, pre_other, forward_token = product(
        "forward_far", "pair", forward, middle + far, pre
    )

    backward = [panel_half, gain]
    panel_own, panel_other, _ = product(
        "backward", "panel", backward, near + middle + far, after=[forward_token]
    )
    with jax.named_scope("pre_acts"):
        received = hop(pre_other, core=1)
    out_rows, out_token = call(
        "out",
        out_kernel, [rows, token], [pre_own, received, acts], [VMEM] * 3
    )
    with jax.named_scope("next_acts"):
        next_acts = shifted(out_rows, 1)

    with jax.named_scope("pre"):
        received = hop(panel_other, core=1)
    with jax.named_scope("restore"):
        restored = hop(panel_half[tokens:], core=1)
    ring_blocks = (RING, CORES, BLOCK, BLOCK)
    keep, send, panel, grads_here = call(
        "units",
        units_kernel,
        [struct(ring_blocks, BF16), struct(ring_blocks, BF16), rows, rows],
        [panel_half, restored, grads],
        [VMEM] * 3,
    )
    (delta,) = call(
        "delta", delta_kernel, [rows], [panel_own, received, grads_here], [VMEM] * 3, after=[keep]
    )
    with jax.named_scope("delta"):
        delta_near, delta_middle, delta_far, take_token = gathered(delta, [out_token])
    with jax.named_scope("stash"):
        stashed = mirrored(acts)

    with jax.named_scope("pair_units"):
        received = hop(send, pair=1)
    mixed, mix_token = call(
        "mix",
        mix_kernel,
        [struct((RING, PAIR, CORES, BLOCK, BLOCK), BF16), token],
        [keep, received],
        [VMEM] * 2,
    )
    units = lax.all_to_all(
        mixed,
        "dp",
        split_axis=0,
        concat_axis=0,
        tiled=True,
        axis_index_groups=[
            [(y * PAIR + x) * CORES + c for y in range(RING)] for x in range(PAIR) for c in range(CORES)
        ],
    )

    with jax.named_scope("delta_other"):
        delta_other = hop(delta, core=1)
    chunks = near + middle + far
    parts, layout = arrays_of(chunks)
    back_own, back_other = call(
        "back",
        functools.partial(back_kernel, layout),
        [back, back],
        [delta, delta_other, *parts],
        [VMEM] * (2 + len(parts)),
        scratch=[pltpu.VMEM((2 * BLOCK, width), BF16)],
        flops=2 * 2 * BLOCK * CHIPS * BLOCK * width,
    )
    with jax.named_scope("back"):
        back_received = hop(back_other, core=1)
    grad_acts, grad_token = call(
        "grads",
        grad_kernel,
        [rows, token],
        [panel, gain, grads_here, back_own, back_received],
        [VMEM] * 5,
        scratch=[pltpu.VMEM((tokens, width), F32)],
    )
    with jax.named_scope("next_grads"):
        next_grads = shifted(grad_acts, -1)
    *outer, near_token = product(
        "outer_near",
        "stacked",
        [units],
        delta_near + delta_middle,
        after=[grad_token],
    )
    parked_out, parked_token = call(
        "park",
        park_kernel,
        [struct(parked.shape, BF16), token],
        [park_slot, kept, stashed],
        [SMEM, ANY, VMEM],
        [ANY, VMEM],
        [pltpu.SemaphoreType.DMA],
        aliases={1: 0},
        after=[near_token],
    )

    outer_own, outer_other, outer_token = product(
        "outer_far", "stacked", [units], delta_far, outer, after=[parked_token, next_grads]
    )
    with jax.named_scope("outer"):
        outer_received = hop(outer_other, core=1)
    next_acts, next_grads, emitted = call(
        "emit",
        emit_kernel,
        [struct((1, tokens, width), BF16), struct((1, tokens, width), BF16), token],
        [next_acts, next_grads],
        [VMEM] * 2,
        after=[outer_token],
    )
    weight_grad, gain_grad = call(
        "finish",
        finish_kernel,
        [struct((1, BLOCK, width), F32), struct((1, BLOCK), F32)],
        [outer_own, outer_received, weight, gain],
        [VMEM] * 4,
        after=[emitted],
    )
    return next_acts, next_grads, parked_out, weight_grad, gain_grad


def solution(mesh):
    return jax.shard_map(
        shards,
        mesh=mesh,
        in_specs=(
            P("section", "dp", None),
            P("section", None),
            P("section", "dp", None),
            P("section", "dp", None),
            P("section", None, "dp", None),
            P(),
            P(),
        ),
        out_specs=(
            P("section", "dp", None),
            P("section", "dp", None),
            P("section", None, "dp", None),
            P("section", "dp", None),
            P("section", "dp"),
        ),
        check_vma=False,
    )
```

```python
import functools

import jax
import jax.numpy as jnp
from jax import lax
from jax.experimental import pallas as pl
from jax.experimental.pallas import tpu as pltpu
from jax.sharding import PartitionSpec as P

EPSILON = 1e-05
RING, PAIR, CORES = 4, 2, 2
CHIPS = RING * PAIR
MEMBERS = CHIPS * CORES
BLOCK = 128
TILE = 1024
MEGABYTES = 12
WIDTH = 2048

VMEM = pl.BlockSpec(memory_space=pltpu.VMEM)
SMEM = pl.BlockSpec(memory_space=pltpu.SMEM)
ANY = pl.BlockSpec(memory_space=pl.ANY)
F32, BF16 = jnp.float32, jnp.bfloat16


def struct(shape, dtype):
    return jax.ShapeDtypeStruct(shape, dtype)


def call(
    name, kernel, outs, args, specs, out_specs=None, scratch=(), flops=0, after=(), aliases=None
):
    nbytes = sum(a.size * a.dtype.itemsize for a in list(args) + list(outs))
    given = len(args)

    def body(*refs):
        kernel(*refs[:given], *refs[given + len(after) :])

    return pl.pallas_call(
        body,
        out_shape=list(outs),
        in_specs=list(specs) + [ANY] * len(after),
        out_specs=list(out_specs) if out_specs else [VMEM] * len(outs),
        scratch_shapes=list(scratch),
        input_output_aliases=aliases or {},
        name=name,
        cost_estimate=pl.CostEstimate(flops=flops, bytes_accessed=nbytes, transcendentals=0),
        compiler_params=pltpu.CompilerParams(vmem_limit_bytes=MEGABYTES * 1024 * 1024),
    )(*args, *after)


def mirrored(block):
    count = lax.axis_size("section")
    return lax.ppermute(block, "section", [(i, count - 1 - i) for i in range(count)])


def shifted(block, distance):
    count = lax.axis_size("section")
    return lax.ppermute(block, "section", [((i - distance) % count, i) for i in range(count)])


def hop(block, ring=0, pair=0, core=0):
    route = []
    for i in range(MEMBERS):
        y, x, c = i // (PAIR * CORES), i // CORES % PAIR, i % CORES
        route.append((i, (((y + ring) % RING) * PAIR + (x ^ pair)) * CORES + (c ^ core)))
    return lax.ppermute(block, "dp", route)


def gathered(own, after=(), take_after=()):
    rows, width = own.shape
    half = rows // 2
    with jax.named_scope("below"):
        below = hop(own, ring=1)
    with jax.named_scope("above"):
        above = hop(own, ring=-1)
    with jax.named_scope("pair"):
        pair = hop(own, pair=1)
    packed = struct((half + rows, width), own.dtype)
    up, down = call(
        "pack",
        pack_kernel,
        [packed, packed],
        [below, above, pair],
        [VMEM] * 3,
        after=after,
    )
    with jax.named_scope("up"):
        up = hop(up, ring=1)
    with jax.named_scope("down"):
        down = hop(down, ring=-1)
    halves = struct((half, width), own.dtype)
    low, high, token = call(
        "take",
        take_kernel,
        [halves, halves, struct((8, BLOCK), F32)],
        [up, down],
        [VMEM] * 2,
        after=take_after,
    )
    with jax.named_scope("far_up"):
        far_up = hop(low, ring=1)
    with jax.named_scope("far_down"):
        far_down = hop(high, ring=-1)
    near = [
        (0, 0, [(own, 0, rows)]),
        (-1, 0, [(below, 0, rows)]),
        (1, 0, [(above, 0, rows)]),
        (0, 1, [(pair, 0, rows)]),
    ]
    middle = [
        (2, 0, [(up, 0, half), (down, rows, rows + half)]),
        (-1, 1, [(up, half, half + rows)]),
        (1, 1, [(down, 0, rows)]),
    ]
    far = [(2, 1, [(far_up, 0, half), (far_down, 0, half)])]
    return near, middle, far, token


def arrays_of(chunks):
    arrays, layout = [], []
    for up, other, pieces in chunks:
        placed = []
        for array, first, last in pieces:
            at = next((i for i, a in enumerate(arrays) if a is array), len(arrays))
            if at == len(arrays):
                arrays.append(array)
            placed.append((at, first, last))
        layout.append((up, other, placed))
    return arrays, layout


def place():
    member = lax.axis_index("dp")
    core = lax.rem(member, CORES)
    return member, core


def chip_of(up, other):
    member = lax.axis_index("dp")
    ring_at = lax.div(member, PAIR * CORES)
    pair_at = lax.rem(lax.div(member, CORES), PAIR)
    pair_to = 1 - pair_at if other else pair_at
    return lax.rem(ring_at + up + RING, RING) * PAIR + pair_to


def columns_of(step):
    return pl.ds(pl.multiple_of(step * TILE, TILE), TILE)


def inverse_rms(values):
    return lax.rsqrt(jnp.mean(values * values, -1, keepdims=True) + EPSILON)


def split_kernel(slots, held, mine, send, panel, sem):
    _, core = place()
    partner = lax.axis_size("section") - 1 - lax.axis_index("section")
    copy = pltpu.make_async_copy(held.at[0, slots[partner]], panel, sem)
    copy.start()
    copy.wait()
    for chip in range(CHIPS):
        at, to = chip * CORES * BLOCK, chip * BLOCK
        first, second = panel[:, at : at + BLOCK], panel[:, at + BLOCK : at + 2 * BLOCK]
        mine[:, to : to + BLOCK] = jnp.where(core == 0, first, second)
        send[:, to : to + BLOCK] = jnp.where(core == 0, second, first)


def join_kernel(mine, received, joined):
    rows = mine.shape[0]
    joined[:rows] = mine[...]
    joined[rows:] = received[...]


def pack_kernel(below, above, pair, up, down):
    rows = pair.shape[0]
    half = rows // 2
    up[:half] = below[:half]
    up[half:] = pair[...]
    down[:rows] = pair[...]
    down[rows:] = above[half:]


def take_kernel(up, down, low, high, token):
    rows = low.shape[0]
    token[...] = jnp.zeros_like(token)
    low[...] = up[rows : 2 * rows]
    high[...] = down[rows : 2 * rows]


def units_kernel(half, received, grads, keep, send, panel, grads_here):
    member, core = place()
    pair_at = lax.rem(lax.div(member, CORES), PAIR)
    grads_here[...] = grads[...]
    rows = received.shape[0]
    for chip in range(CHIPS):
        at, of = chip * CORES * BLOCK, chip * BLOCK
        own, other = half[:rows, of : of + BLOCK], received[:, of : of + BLOCK]
        panel[:, at : at + BLOCK] = jnp.where(core == 0, own, other)
        panel[:, at + BLOCK : at + 2 * BLOCK] = jnp.where(core == 0, other, own)
    values = panel[...].astype(F32)
    unit = values * inverse_rms(values)
    for y in range(RING):
        blocks = []
        for block in range(PAIR * CORES):
            at = (y * PAIR * CORES + block) * BLOCK
            blocks.append(jnp.transpose(unit[:, at : at + BLOCK]).astype(BF16))
        for c in range(CORES):
            mine = [jnp.where(core == 0, blocks[x + c], blocks[x + 1 - c]) for x in (0, CORES)]
            keep[y, c] = jnp.where(pair_at == 0, mine[0], mine[1])
            send[y, c] = jnp.where(pair_at == 0, mine[1], mine[0])


def mix_kernel(keep, received, mixed, token):
    token[...] = jnp.zeros_like(token)
    for y in range(RING):
        mixed[y, 0] = keep[y]
        mixed[y, 1] = received[y]


def normed_kernel(rows, gain, mine, send):
    _, core = place()
    values = rows[...].astype(F32)
    unit = values * inverse_rms(values)
    normed = (unit * gain[...]).astype(BF16)
    for chip in range(CHIPS):
        at = chip * CORES * BLOCK
        first, second = normed[:, at : at + BLOCK], normed[:, at + BLOCK : at + 2 * BLOCK]
        mine[chip] = jnp.where(core == 0, first, second)
        send[chip] = jnp.where(core == 0, second, first)


def product_kernel(layout, kind, added, *refs):
    refs = list(refs)
    left, token = refs.pop(), refs.pop(-1)
    token[...] = jnp.zeros_like(token)
    out_own, out_other = refs[-2:]
    del refs[-2:]
    _, core = place()
    first_ref, second_ref = refs.pop(0), None if kind == "stacked" else refs.pop(0)
    totals = [refs.pop(), refs.pop()][::-1] if added else None
    for k, (up, to_other, _) in enumerate(layout):
        chip = chip_of(up, to_other)
        columns = slice(k * BLOCK, (k + 1) * BLOCK)
        if kind == "stacked":
            left[:BLOCK, columns] = first_ref[lax.div(chip, PAIR), to_other, 0]
            left[BLOCK:, columns] = first_ref[lax.div(chip, PAIR), to_other, 1]
        elif kind == "pair":
            left[:BLOCK, columns] = first_ref[chip]
            left[BLOCK:, columns] = second_ref[chip]
        else:
            at = pl.ds(pl.multiple_of(chip * BLOCK, BLOCK), BLOCK)
            of = pl.ds(pl.multiple_of((chip * CORES + core) * BLOCK, BLOCK), BLOCK)
            left[:, columns] = (first_ref[:, at].astype(F32) * second_ref[:, of]).astype(BF16)

    @pl.loop(0, WIDTH // TILE)
    def _(step):
        columns = columns_of(step)
        right = jnp.concatenate(
            [refs[i][first:last, columns] for _, _, placed in layout for i, first, last in placed], 0
        )
        result = jnp.dot(left[...], right, preferred_element_type=F32)
        low, high = result[:BLOCK], result[BLOCK:]
        if added:
            low, high = low + totals[0][:, columns], high + totals[1][:, columns]
        out_own[:, columns] = low
        out_other[:, columns] = high.astype(out_other.dtype)

    if kind == "panel":
        values = first_ref[...].astype(F32)
        squares = jnp.broadcast_to(jnp.sum(values * values, -1, keepdims=True), (2 * BLOCK, BLOCK))
        out_own[:, WIDTH:] = squares[:BLOCK]
        rounded = squares[BLOCK:].astype(BF16)
        out_other[:, WIDTH : WIDTH + BLOCK] = rounded
        out_other[:, WIDTH + BLOCK :] = (squares[BLOCK:] - rounded.astype(F32)).astype(BF16)


def product(name, kind, blocks, chunks, totals=(), after=()):
    parts, layout = arrays_of(chunks)
    depth, width = len(chunks) * BLOCK, WIDTH + (BLOCK if kind == "panel" else 0)
    last = struct((BLOCK, width + (BLOCK if kind == "panel" else 0)), BF16)
    args = [*blocks, *parts, *totals]
    out = struct((BLOCK, width), F32)
    return call(
        name,
        functools.partial(product_kernel, layout, kind, bool(totals)),
        [out, last if totals or kind == "panel" else out, struct((8, BLOCK), F32)],
        args,
        [VMEM] * len(args),
        scratch=[pltpu.VMEM((2 * BLOCK, depth), BF16)],
        flops=2 * 2 * BLOCK * depth * width,
        after=after,
    )


def delta_kernel(own, received, grads, delta):
    squares = own[:, WIDTH : WIDTH + 1] + (
        received[:, WIDTH : WIDTH + 1].astype(F32)
        + received[:, WIDTH + BLOCK : WIDTH + BLOCK + 1].astype(F32)
    )
    inverse = lax.rsqrt(squares * (1.0 / WIDTH) + EPSILON)

    @pl.loop(0, WIDTH // TILE)
    def _(step):
        columns = columns_of(step)
        pre_act = (own[:, columns] + received[:, columns].astype(F32)) * inverse
        sigma = jax.nn.sigmoid(pre_act)
        grad_f = grads[:, columns].astype(F32)
        delta[:, columns] = (grad_f * sigma * (1.0 + pre_act * (1.0 - sigma))).astype(BF16)


def out_kernel(own, received, acts, out, token):
    token[...] = jnp.zeros_like(token)

    @pl.loop(0, out.shape[1] // TILE)
    def _(step):
        columns = columns_of(step)
        pre_act = own[:, columns] + received[:, columns].astype(F32)
        values = acts[:, columns].astype(F32)
        out[:, columns] = (values + pre_act * jax.nn.sigmoid(pre_act)).astype(BF16)


def back_kernel(layout, delta_own, delta_other, *refs):
    refs = list(refs)
    left = refs.pop()
    back_own, back_other = refs[-2:]
    left[:BLOCK] = delta_own[...]
    left[BLOCK:] = delta_other[...]
    for k in range(0, len(layout), 2):
        right = jnp.concatenate(
            [refs[i][first:last] for _, _, placed in layout[k : k + 2] for i, first, last in placed], 0
        )
        result = lax.dot_general(
            left[...], right, (((1,), (1,)), ((), ())), preferred_element_type=F32
        )
        for i, (up, other, _) in enumerate(layout[k : k + 2]):
            chip = chip_of(up, other)
            back_own[chip] = result[:BLOCK, i * BLOCK : (i + 1) * BLOCK]
            back_other[chip] = result[BLOCK:, i * BLOCK : (i + 1) * BLOCK]


def grad_kernel(panel, gain, grads, back_own, back_received, grad_acts, token, through):
    token[...] = jnp.zeros_like(token)
    _, core = place()
    values = panel[...].astype(F32)
    inverse = inverse_rms(values)
    for chip in range(CHIPS):
        at = chip * CORES * BLOCK
        own, received = back_own[chip], back_received[chip]
        through[:, at : at + BLOCK] = jnp.where(core == 0, own, received)
        through[:, at + BLOCK : at + 2 * BLOCK] = jnp.where(core == 0, received, own)
    unit = values * inverse
    scaled = through[...] * gain[...]
    mean = jnp.mean(scaled * unit, -1, keepdims=True)
    grad_acts[...] = (grads[...].astype(F32) + inverse * (scaled - unit * mean)).astype(BF16)


def keep_kernel(held, out, token, sem):
    copy = pltpu.make_async_copy(held, out, sem)
    copy.start()
    token[...] = jnp.zeros_like(token)
    copy.wait()


def park_kernel(slots, kept, stashed, out, token, sem):
    del kept
    partner = lax.axis_size("section") - 1 - lax.axis_index("section")
    copy = pltpu.make_async_copy(stashed, out.at[0, slots[partner]], sem)
    copy.start()
    token[...] = jnp.zeros_like(token)
    copy.wait()


def emit_kernel(acts, grads, next_acts, next_grads, token):
    next_acts[0] = acts[...]
    next_grads[0] = grads[...]
    token[...] = jnp.zeros_like(token)


def finish_kernel(own, received, weight, gain, weight_grad, gain_grad):
    member, _ = place()
    own_gain = gain[:, pl.ds(pl.multiple_of(member * BLOCK, BLOCK), BLOCK)]
    scale = jnp.transpose(jnp.broadcast_to(own_gain, (BLOCK, BLOCK)))[:, :1]
    total = jnp.zeros((BLOCK, 1), F32)
    for at in range(0, own.shape[1], TILE):
        outer = own[:, at : at + TILE] + received[:, at : at + TILE].astype(F32)
        weight_grad[0, :, at : at + TILE] = outer * scale
        total += jnp.sum(outer * weight[0, :, at : at + TILE].astype(F32), -1, keepdims=True)
    gain_grad[...] = jnp.transpose(jnp.broadcast_to(total, (BLOCK, BLOCK)))[:1]


def shards(weight, gain, acts_in, grads_in, parked, fetch_slot, park_slot):
    tokens, width = acts_in.shape[1:]
    acts, grads = acts_in[0], grads_in[0]
    rows, blocks = struct((tokens, width), BF16), struct((CHIPS, BLOCK, BLOCK), BF16)
    token = struct((8, BLOCK), F32)
    back = struct((CHIPS, BLOCK, BLOCK), F32)

    half = struct((tokens, width // CORES), BF16)
    mine, send = call(
        "split",
        split_kernel,
        [half, half],
        [fetch_slot, parked],
        [SMEM, ANY],
        scratch=[pltpu.VMEM((tokens, width), BF16), pltpu.SemaphoreType.DMA],
    )
    (joined,) = call(
        "join",
        join_kernel,
        [struct((2 * tokens, width // CORES), BF16)],
        [mine, hop(send, core=1)],
        [VMEM] * 2,
    )
    with jax.named_scope("panel"):
        panel_half = mirrored(joined)
    mine, send = call("norm_acts", normed_kernel, [blocks, blocks], [acts, gain], [VMEM] * 2)
    kept, kept_token = call(
        "keep",
        keep_kernel,
        [struct(parked.shape, BF16), token],
        [parked],
        [VMEM],
        [ANY, VMEM],
        [pltpu.SemaphoreType.DMA],
        after=[joined],
    )
    with jax.named_scope("weight"):
        near, middle, far, _ = gathered(weight[0], after=[joined, mine, kept_token])

    with jax.named_scope("acts"):
        forward = [mine, hop(send, core=1)]
    *pre, _ = product("forward_near", "pair", forward, near)
    pre_own, pre_other, forward_token = product(
        "forward_far", "pair", forward, middle + far, pre
    )

    backward = [panel_half, gain]
    panel_own, panel_other, _ = product(
        "backward", "panel", backward, near + middle + far, after=[forward_token]
    )
    with jax.named_scope("pre_acts"):
        received = hop(pre_other, core=1)
    out_rows, out_token = call(
        "out",
        out_kernel, [rows, token], [pre_own, received, acts], [VMEM] * 3
    )
    with jax.named_scope("next_acts"):
        next_acts = shifted(out_rows, 1)

    with jax.named_scope("pre"):
        received = hop(panel_other, core=1)
    with jax.named_scope("restore"):
        restored = hop(panel_half[tokens:], core=1)
    ring_blocks = (RING, CORES, BLOCK, BLOCK)
    keep, send, panel, grads_here = call(
        "units",
        units_kernel,
        [struct(ring_blocks, BF16), struct(ring_blocks, BF16), rows, rows],
        [panel_half, restored, grads],
        [VMEM] * 3,
    )
    (delta,) = call(
        "delta", delta_kernel, [rows], [panel_own, received, grads_here], [VMEM] * 3, after=[keep]
    )
    with jax.named_scope("delta"):
        delta_near, delta_middle, delta_far, take_token = gathered(delta, [out_token])
    with jax.named_scope("stash"):
        stashed = mirrored(acts)

    with jax.named_scope("pair_units"):
        received = hop(send, pair=1)
    mixed, mix_token = call(
        "mix",
        mix_kernel,
        [struct((RING, PAIR, CORES, BLOCK, BLOCK), BF16), token],
        [keep, received],
        [VMEM] * 2,
    )
    units = lax.all_to_all(
        mixed,
        "dp",
        split_axis=0,
        concat_axis=0,
        tiled=True,
        axis_index_groups=[
            [(y * PAIR + x) * CORES + c for y in range(RING)] for x in range(PAIR) for c in range(CORES)
        ],
    )

    with jax.named_scope("delta_other"):
        delta_other = hop(delta, core=1)
    chunks = near + middle + far
    parts, layout = arrays_of(chunks)
    back_own, back_other = call(
        "back",
        functools.partial(back_kernel, layout),
        [back, back],
        [delta, delta_other, *parts],
        [VMEM] * (2 + len(parts)),
        scratch=[pltpu.VMEM((2 * BLOCK, width), BF16)],
        flops=2 * 2 * BLOCK * CHIPS * BLOCK * width,
    )
    with jax.named_scope("back"):
        back_received = hop(back_other, core=1)
    grad_acts, grad_token = call(
        "grads",
        grad_kernel,
        [rows, token],
        [panel, gain, grads_here, back_own, back_received],
        [VMEM] * 5,
        scratch=[pltpu.VMEM((tokens, width), F32)],
    )
    with jax.named_scope("next_grads"):
        next_grads = shifted(grad_acts, -1)
    *outer, near_token = product(
        "outer_near",
        "stacked",
        [units],
        delta_near + delta_middle,
        after=[grad_token],
    )
    parked_out, parked_token = call(
        "park",
        park_kernel,
        [struct(parked.shape, BF16), token],
        [park_slot, kept, stashed],
        [SMEM, ANY, VMEM],
        [ANY, VMEM],
        [pltpu.SemaphoreType.DMA],
        aliases={1: 0},
        after=[near_token],
    )

    outer_own, outer_other, outer_token = product(
        "outer_far", "stacked", [units], delta_far, outer, after=[parked_token, next_grads]
    )
    with jax.named_scope("outer"):
        outer_received = hop(outer_other, core=1)
    next_acts, next_grads, emitted = call(
        "emit",
        emit_kernel,
        [struct((1, tokens, width), BF16), struct((1, tokens, width), BF16), token],
        [next_acts, next_grads],
        [VMEM] * 2,
        after=[outer_token],
    )
    weight_grad, gain_grad = call(
        "finish",
        finish_kernel,
        [struct((1, BLOCK, width), F32), struct((1, BLOCK), F32)],
        [outer_own, outer_received, weight, gain],
        [VMEM] * 4,
        after=[emitted],
    )
    return next_acts, next_grads, parked_out, weight_grad, gain_grad


def solution(mesh):
    return jax.shard_map(
        shards,
        mesh=mesh,
        in_specs=(
            P("section", "dp", None),
            P("section", None),
            P("section", "dp", None),
            P("section", "dp", None),
            P("section", None, "dp", None),
            P(),
            P(),
        ),
        out_specs=(
            P("section", "dp", None),
            P("section", "dp", None),
            P("section", None, "dp", None),
            P("section", "dp", None),
            P("section", "dp"),
        ),
        check_vma=False,
    )
```
